256 devices in a mesh: tm: 8 (over x, core), height: 16 (over z, y_hi), dp: 2 (over y_lo).
Axes of the slice: x: 4, y: 4 (y_hi: 2, y_lo: 2; y = y_hi * 2 + y_lo), z: 8, core: 2. Of those that a mesh axis runs over, the one named last changes fastest.
Arguments:
- video_clip: bfloat16 [2, 16, 64, 32, 256], P('dp', 'tm', 'height'), may hold values from -6 to 6
- conv_weight: bfloat16 [3, 3, 3, 256, 256], replicated, may hold values from -0.078125 to 0.078125
- down_weight: bfloat16 [3, 3, 3, 256, 256], replicated, may hold values from -0.078125 to 0.078125
- output_grad: bfloat16 [2, 8, 32, 16, 256], P('dp', 'tm', 'height'), may hold values from -12 to 12
Outputs:
- encoded: bfloat16 [2, 8, 32, 16, 256], P('dp', 'tm', 'height')
- clip_grad: bfloat16 [2, 16, 64, 32, 256], P('dp', 'tm', 'height')
- conv_grad: float32 [6912, 256], P(('height', 'dp'))
- down_grad: float32 [6912, 256], P(('height', 'dp'))
The draws below stay inside these ranges and needn't reach their ends.
All inputs are finite; a program needn't handle non-finite values.
Results may differ from the reference program's by a relative error of at most 0.005.
Values may be sent and summed in bfloat16 or wider, within the bound.
A program may use at most 128 MiB of HBM per device.

```python
import math
import jax
import jax.numpy as jnp

C = 256
COLS = 32
CLIPS = 2
FRAMES = 16
ROWS = 64


def level_of(own_key, shape, shards, least, largest):
    level = 1.0
    for dim, shards_of in shards:
        heights = jax.random.uniform(jax.random.fold_in(jax.random.fold_in(own_key, 6), dim), (shards_of,), jnp.float32, least / len(shards), largest / len(shards))
        level = level * jnp.repeat(jnp.exp(heights), shape[dim] // shards_of).reshape((-1,) + (1,) * (len(shape) - 1 - dim))
    return level


def noise(own_key, extent, spread, reach, cuts=(), kind=jnp.bfloat16):
    entries = spread * jax.random.normal(own_key, extent, jnp.float32)
    if cuts:
        entries = entries * level_of(own_key, extent, cuts, -0.22, 0.18)
    return jnp.clip(entries, -reach, reach).astype(kind)


def setup_inputs(seed: int = 0) -> dict:
    keys = jax.random.split(jax.random.key(seed), 5)
    return {
        "video_clip": noise(keys[0], (CLIPS, FRAMES, ROWS, COLS, C), 1.0, 6.0, ((0, 2), (1, 8), (2, 16))),
        "conv_weight": noise(keys[1], (3, 3, 3, C, C), (27 * C) ** -0.5, 0.078125),
        "down_weight": noise(keys[2], (3, 3, 3, C, C), (27 * C) ** -0.5, 0.078125),
        "output_grad": noise(keys[3], (CLIPS, FRAMES // 2, ROWS // 2, COLS // 2, C), 2.0, 12.0, ((0, 2), (1, 8), (2, 16))),
    }


def window_of(padded, time_tap, row_tap, stride, frame_count, row_count, column_count):
    pieces = [padded[time_tap:time_tap + stride * frame_count:stride, row_tap:row_tap + stride * row_count:stride, column_tap:column_tap + stride * column_count:stride] for column_tap in range(3)]
    return jnp.concatenate(pieces, axis=-1).reshape(frame_count * row_count * column_count, -1)

def tap_conv(padded, weight, stride, frame_count, row_count, column_count):
    channels = weight.shape[-1]
    accumulated = jnp.zeros((frame_count * row_count * column_count, channels), jnp.float32)
    for time_tap in range(3):
        for row_tap in range(3):
            window = window_of(padded, time_tap, row_tap, stride, frame_count, row_count, column_count)
            accumulated = accumulated + jnp.dot(window, weight[time_tap, row_tap].reshape(3 * channels, channels), preferred_element_type=jnp.float32)
    return accumulated.reshape(frame_count, row_count, column_count, channels)

def weight_terms(padded, grad_rows, stride, frame_count, row_count, column_count):
    blocks = []
    for time_tap in range(3):
        for row_tap in range(3):
            window = window_of(padded, time_tap, row_tap, stride, frame_count, row_count, column_count)
            blocks.append(jnp.dot(window.T, grad_rows, preferred_element_type=jnp.float32))
    return jnp.concatenate(blocks, axis=0)

def spread_back(grad_rows, weight, stride, shape, frame_count, row_count, column_count):
    channels = weight.shape[-1]
    result = jnp.zeros(shape, jnp.float32)
    for time_tap in range(3):
        for row_tap in range(3):
            product = jnp.dot(grad_rows, weight[time_tap, row_tap].reshape(3 * channels, channels).T, preferred_element_type=jnp.float32)
            product = product.reshape(frame_count, row_count, column_count, 3, channels)
            for column_tap in range(3):
                result = result.at[time_tap:time_tap + stride * frame_count:stride, row_tap:row_tap + stride * row_count:stride, column_tap:column_tap + stride * column_count:stride].add(product[:, :, :, column_tap])
    return result

def clip_pass(frames_in, conv_weight, down_weight, output_grad):
    frame_count, row_count, column_count, channels = frames_in.shape
    half_frames = frame_count // 2
    half_rows = row_count // 2
    half_columns = column_count // 2
    extended = jnp.concatenate([frames_in[:1], frames_in[:1], frames_in], axis=0)
    padded_in = jnp.pad(extended, ((0, 0), (1, 1), (1, 1), (0, 0)))
    before = tap_conv(padded_in, conv_weight, 1, frame_count, row_count, column_count)
    hidden = jax.nn.silu(before).astype(jnp.bfloat16)
    extended_hidden = jnp.concatenate([hidden[:1], hidden[:1], hidden], axis=0)
    padded_hidden = jnp.pad(extended_hidden, ((0, 0), (0, 1), (0, 1), (0, 0)))
    encoded = tap_conv(padded_hidden, down_weight, 2, half_frames, half_rows, half_columns).astype(jnp.bfloat16)
    grad_rows = output_grad.reshape(-1, channels)
    down_terms = weight_terms(padded_hidden, grad_rows, 2, half_frames, half_rows, half_columns)
    padded_grad = spread_back(grad_rows, down_weight, 2, padded_hidden.shape, half_frames, half_rows, half_columns)
    hidden_grad = padded_grad[2:, :row_count, :column_count]
    hidden_grad = hidden_grad.at[0].add(padded_grad[0, :row_count, :column_count] + padded_grad[1, :row_count, :column_count])
    sigmoid = jax.nn.sigmoid(before)
    before_grad = (hidden_grad * (sigmoid * (1.0 + before * (1.0 - sigmoid)))).astype(jnp.bfloat16)
    before_rows = before_grad.reshape(-1, channels)
    conv_terms = weight_terms(padded_in, before_rows, 1, frame_count, row_count, column_count)
    padded_in_grad = spread_back(before_rows, conv_weight, 1, padded_in.shape, frame_count, row_count, column_count)
    clip_grad = padded_in_grad[2:, 1:-1, 1:-1]
    clip_grad = clip_grad.at[0].add(padded_in_grad[0, 1:-1, 1:-1] + padded_in_grad[1, 1:-1, 1:-1])
    return (encoded, clip_grad.astype(jnp.bfloat16), conv_terms, down_terms)

def reference(video_clip, conv_weight, down_weight, output_grad):
    encoded_list = []
    grad_list = []
    conv_total = jnp.zeros((27 * C, C), jnp.float32)
    down_total = jnp.zeros((27 * C, C), jnp.float32)
    for clip_index in range(CLIPS):
        encoded, clip_grad, conv_terms, down_terms = clip_pass(video_clip[clip_index], conv_weight, down_weight, output_grad[clip_index])
        encoded_list.append(encoded)
        grad_list.append(clip_grad)
        conv_total = conv_total + conv_terms
        down_total = down_total + down_terms
    conv_scale = 1.0 / math.sqrt(CLIPS * FRAMES * ROWS * COLS)
    down_scale = 1.0 / math.sqrt(CLIPS * FRAMES * ROWS * COLS // 8)
    return (jnp.stack(encoded_list), jnp.stack(grad_list), conv_total * conv_scale, down_total * down_scale)
```

```python
import functools
import math

import jax
import jax.numpy as jnp
from jax import lax
from jax.experimental import pallas as pl
from jax.experimental.pallas import tpu as pltpu
from jax.sharding import PartitionSpec as P

MESH = pl.DeviceIdType.MESH
F32 = jnp.float32
BF16 = jnp.bfloat16
NT = (((1,), (1,)), ((), ()))
TN = (((0,), (0,)), ((), ()))


def iota2(shape, dim):
    return lax.broadcasted_iota(jnp.int32, shape, dim)


def one_hot(mask):
    return jnp.where(mask, 1.0, 0.0).astype(F32).astype(BF16)


def column_order(n):
    m, k = iota2((n, n), 0), iota2((n, n), 1)
    return one_hot(k == (m & ~31) + 2 * (m & 15) + ((m >> 4) & 1))


def channel_order(n):
    i, k = iota2((n, n), 0), iota2((n, n), 1)
    j = k & 127
    return one_hot(i == (j >> 3) * 16 + (k >> 7) * 8 + (j & 7))


def move_in_16(x, step):
    n = x.shape[0]
    k = iota2(x.shape, 0) & 15
    rolled = pltpu.roll(x, step % n, 0)
    return jnp.where(k == (0 if step == 1 else 15), 0.0, rolled)


def halves(x):
    groups = x.shape[0] // 32
    parts = x.reshape(groups, 2, 16, x.shape[1])
    return parts[:, 0].reshape(groups * 16, -1), parts[:, 1].reshape(groups * 16, -1)


def joined(even, odd):
    groups = even.shape[0] // 16
    parts = [h.reshape(groups, 1, 16, h.shape[1]) for h in (even, odd)]
    return jnp.concatenate(parts, axis=1).reshape(groups * 32, -1)


def from_left(x):
    even, odd = halves(x)
    return joined(move_in_16(odd, 1), even)


def from_right(x):
    even, odd = halves(x)
    return joined(odd, move_in_16(even, -1))


def kernel(
    sizes,
    x_ref, w1_hbm, w2_hbm, og_ref,
    enc_ref, clip_ref, conv_ref, down_ref,
    w1, w2, xe, oge, he, ge, hg, before, zs,
    xs, gs, hs, os_, xg, gg, hgat, ogat, xt, g3, part,
    sl, r1, s1, r2, fs, fg, ff,
    wsem, p1s, p1r, p2s, p2r,
    xss, xsr, gss, gsr, hss, hsr, oss, osr,
    rs1s, rs1r, rs2s, rs2r, ags, agr,
):
    nt, nh, nd = sizes
    ny, nz = 2 * nd, nh // 2
    t, h, d = lax.axis_index("tm"), lax.axis_index("height"), lax.axis_index("dp")
    y, z = (h % 2) * nd + d, h // 2
    core, chip = t % 2, t // 2
    t_next, t_prev = (t + 1) % nt, (t + nt - 1) % nt
    h_next, h_prev = (h + 1) % nh, (h + nh - 1) % nh
    block = z * ny + y
    groups = 864 // (ny * nz)
    slot = 8 * ((groups + 1) // 2)

    wc1 = pltpu.make_async_copy(w1_hbm, w1, wsem.at[0])
    wc2 = pltpu.make_async_copy(w2_hbm, w2, wsem.at[1])
    wc2.start()
    wc1.start()

    def at_y(k):
        return (t, z * 2 + k // nd, k % nd)

    barrier = pltpu.get_barrier_semaphore()

    def greet(where):
        pl.semaphore_signal(barrier, inc=1, device_id=where, device_id_type=MESH)

    for k in range(1, nt):
        greet(((t + k) % nt, h, d))
    for hh in (h_next, h_prev):
        for tt in (t_prev, t, t_next):
            greet((tt, hh, d))
    for k in range(1, ny):
        greet(at_y((y + k) % ny))
    for k in range(1, nz):
        greet((t, ((z + k) % nz) * 2 + h % 2, d))

    x_own = jnp.dot(column_order(256), x_ref[...], preferred_element_type=F32).astype(BF16)
    xe[2:4, 1:5] = x_own.reshape(2, 4, 32, 256)
    oge[0, 1:3] = og_ref[...].reshape(2, 16, 256)
    for k in range(2):
        os_[k] = og_ref[:, 128 * k : 128 * (k + 1)].reshape(2, 16, 128)

    pl.semaphore_wait(barrier, (nt - 1) + 6 + (ny - 1) + (nz - 1))

    def send(src, dst, ssem, rsem, where):
        return pltpu.make_async_remote_copy(
            src_ref=src, dst_ref=dst, send_sem=ssem, recv_sem=rsem, device_id=where, device_id_type=MESH
        )

    def p1(k, src, dst, where):
        return send(src, dst, p1s.at[k], p1r.at[k], where)

    og_halo = [
        p1(0, oge.at[0:1, 1:3], oge.at[1:2, 1:3], (t_prev, h, d)),
        p1(1, oge.at[0:1, 2:3], oge.at[0:1, 0:1], (t, h_next, d)),
        p1(2, oge.at[0:1, 2:3], oge.at[1:2, 0:1], (t_prev, h_next, d)),
    ]
    x_halo = [
        p1(3, xe.at[2:4, 1:5], xe.at[0:2, 1:5], (t_next, h, d)),
        p1(4, xe.at[2:4, 4:5], xe.at[2:4, 0:1], (t, h_next, d)),
        p1(5, xe.at[2:4, 1:2], xe.at[2:4, 5:6], (t, h_prev, d)),
        p1(6, xe.at[2:4, 4:5], xe.at[0:2, 0:1], (t_next, h_next, d)),
        p1(7, xe.at[2:4, 1:2], xe.at[0:2, 5:6], (t_next, h_prev, d)),
    ]
    for c in og_halo + x_halo:
        c.start()

    def gather_sends(role, source, target, ssem, rsem):
        for k in range(nt // 2):
            to_chip = (chip + k) % (nt // 2)
            to = to_chip * 2 + role
            c = send(source(to_chip), target(t), ssem.at[k], rsem.at[t], (to, h, d))
            if k == 0:
                pl.when(core != role)(c.start)
            else:
                c.start()

    def gather_sent(role, source, target, ssem, rsem):
        for k in range(nt // 2):
            to_chip = (chip + k) % (nt // 2)
            c = send(source(to_chip), target(t), ssem.at[k], rsem.at[t], (to_chip * 2 + role, h, d))
            if k == 0:
                pl.when(core != role)(c.wait_send)
            else:
                c.wait_send()

    def gather_received(source, target, ssem, rsem):
        for k in range(1, nt):
            s = (t + k) % nt
            send(source(0), target(s), ssem.at[0], rsem.at[s], (s, h, d)).wait_recv()

    og_move = (lambda c: os_.at[c % 2], lambda s: ogat.at[s], oss, osr)
    x_move = (lambda c: xs.at[c // 2], lambda s: xg.at[pl.ds(2 + 2 * s, 2)], xss, xsr)
    g_move = (lambda c: gs.at[c % 2], lambda s: gg.at[pl.ds(2 * s, 2)], gss, gsr)
    h_move = (lambda c: hs.at[c // 2], lambda s: hgat.at[pl.ds(2 + 2 * s, 2)], hss, hsr)
    gather_sends(1, *og_move)

    wc2.wait()
    for c in og_halo:
        c.wait_recv()

    @pl.when(t == nt - 1)
    def _():
        oge[1] = jnp.zeros((3, 16, 256), BF16)

    @pl.when(h == 0)
    def _():
        oge[:, 0] = jnp.zeros((2, 16, 256), BF16)

    og_rows = oge[...].reshape(96, 256)
    first = t == 0
    terms = {}
    for e in range(3):
        for a in range(3):
            for b in range(3):
                lhs = og_rows if a < 2 else og_rows[:48]
                q = lax.dot_general(lhs, w2[a * 9 + b * 3 + e], NT, preferred_element_type=F32)
                offset = 0 if b == 2 else 16
                here = q[offset : offset + 32]
                if a < 2:
                    here = jnp.where(first, here, 0.0)
                    later = q[48 + offset : 48 + offset + 32]
                    key = (a, b % 2, e)
                    terms[key] = terms.get(key, 0.0) + later
                key = (0, b % 2, e)
                terms[key] = terms.get(key, 0.0) + here
    for f in range(2):
        for b in range(2):
            even = terms[f, b, 0] + move_in_16(terms[f, b, 2], 1)
            odd = terms[f, b, 1]
            for u in range(2):
                hg[f, 2 * u + b, 0:16] = even[16 * u : 16 * u + 16]
                hg[f, 2 * u + b, 16:32] = odd[16 * u : 16 * u + 16]

    for c in x_halo:
        c.wait_recv()

    @pl.when(h == 0)
    def _():
        xe[:, 0] = jnp.zeros((4, 32, 256), BF16)

    @pl.when(h == nh - 1)
    def _():
        xe[:, 5] = jnp.zeros((4, 32, 256), BF16)

    @pl.when(first)
    def _():
        xe[0] = xe[2]
        xe[1] = xe[2]

    by_channel = channel_order(256)
    moved = jnp.dot(xe[2:4].reshape(384, 256), by_channel, preferred_element_type=F32).astype(BF16)
    for k in range(2):
        xs[k] = moved[:, 128 * k : 128 * (k + 1)].reshape(2, 6, 32, 128)
    gather_sends(0, *x_move)

    wc1.wait()
    sums = [None] * 3
    for a in range(3):
        for b in range(3):
            lhs = xe[a : a + 2, b : b + 4].reshape(256, 256)
            for e in range(3):
                q = jnp.dot(lhs, w1[a * 9 + b * 3 + e], preferred_element_type=F32)
                sums[e] = q if sums[e] is None else sums[e] + q
    value = from_left(sums[0]) + sums[1] + from_right(sums[2])
    sigmoid = jax.nn.sigmoid(value)
    he[2:4, 0:4] = (value * sigmoid).astype(BF16).reshape(2, 4, 32, 256)
    slope = sigmoid * (1.0 + value * (1.0 - sigmoid))
    grad = (hg[...].reshape(256, 256) * slope).astype(BF16)
    ge[0:2, 1:5] = grad.reshape(2, 4, 32, 256)
    for k in range(2):
        gs[k] = grad[:, 128 * k : 128 * (k + 1)].reshape(2, 4, 32, 128)

    def p2(k, src, dst, where):
        return send(src, dst, p2s.at[k], p2r.at[k], where)

    h_rows = p2(0, he.at[2:4, 0:1], he.at[2:4, 4:5], (t, h_prev, d))
    h_halo = [
        p2(1, he.at[2:4, 0:1], he.at[0:2, 4:5], (t_next, h_prev, d)),
        p2(2, he.at[2:4, 0:4], he.at[0:2, 0:4], (t_next, h, d)),
    ]
    g_halo = [
        p2(3, ge.at[0:2, 1:5], ge.at[2:4, 1:5], (t_prev, h, d)),
        p2(4, ge.at[0:2, 4:5], ge.at[0:2, 0:1], (t, h_next, d)),
        p2(5, ge.at[0:2, 1:2], ge.at[0:2, 5:6], (t, h_prev, d)),
        p2(6, ge.at[0:2, 4:5], ge.at[2:4, 0:1], (t_prev, h_next, d)),
        p2(7, ge.at[0:2, 1:2], ge.at[2:4, 5:6], (t_prev, h_prev, d)),
    ]
    h_rows.start()
    gather_sends(0, *g_move)
    for c in h_halo + g_halo:
        c.start()
    h_rows.wait_recv()

    @pl.when(h == nh - 1)
    def _():
        he[2:4, 4] = jnp.zeros((2, 32, 256), BF16)

    moved = jnp.dot(he[2:4].reshape(320, 256), by_channel, preferred_element_type=F32).astype(BF16)
    for k in range(2):
        hs[k] = moved[:, 128 * k : 128 * (k + 1)].reshape(2, 5, 32, 128)
    gather_sends(1, *h_move)

    for c in h_halo:
        c.wait_recv()

    @pl.when(h == nh - 1)
    def _():
        he[0:2, 4] = jnp.zeros((2, 32, 256), BF16)

    @pl.when(first)
    def _():
        he[0] = he[2]
        he[1] = he[2]

    sums = [None] * 3
    for a in range(3):
        for b in range(3):
            for e in range(3):
                p = 16 * (e % 2)
                lhs = jnp.concatenate([he[a, b, p : p + 16], he[a, b + 2, p : p + 16]], axis=0)
                q = jnp.dot(lhs, w2[a * 9 + b * 3 + e], preferred_element_type=F32)
                sums[e] = q if sums[e] is None else sums[e] + q
    enc_ref[...] = (sums[0] + sums[1] + move_in_16(sums[2], -1)).astype(BF16)

    part[pl.ds(27 * 128, 8)] = jnp.zeros((8, 128), F32)

    @pl.when(core == 0)
    def _():
        xg[pl.ds(2 + 2 * t, 2)] = xs[chip // 2]
        gg[pl.ds(2 * t, 2)] = gs[chip % 2]
        gather_received(*x_move)
        xg[0] = xg[2]
        xg[1] = xg[2]

        def turn(f, carry):
            for b in range(3):
                xt[f, 128 * b : 128 * (b + 1)] = xg[f, b : b + 4].reshape(128, 128).T
            return carry

        lax.fori_loop(0, 2 * nt + 2, turn, 0)
        gather_received(*g_move)

        def spread(s, carry):
            rows = pl.ds(pl.multiple_of(256 * s, 256), 256)
            g = gg[pl.ds(2 * s, 2)].reshape(256, 128)
            wide = g.astype(F32)
            g3[rows, 0:128] = from_right(wide).astype(BF16)
            g3[rows, 128:256] = g
            g3[rows, 256:384] = from_left(wide).astype(BF16)
            return carry

        lax.fori_loop(0, nt, spread, 0)
        for a in range(3):
            lhs = jnp.concatenate([xt[a + f] for f in range(2 * nt)], axis=1)
            q = jnp.dot(lhs, g3[...], preferred_element_type=F32)
            for b in range(3):
                for e in range(3):
                    n = 128 * (a * 9 + b * 3 + e)
                    part[n : n + 128] = q[128 * b : 128 * (b + 1), 128 * e : 128 * (e + 1)]

    @pl.when(core == 1)
    def _():
        hgat[pl.ds(2 + 2 * t, 2)] = hs[chip // 2]
        ogat[t] = os_[chip % 2]
        gather_received(*og_move)
        gather_received(*h_move)
        hgat[0] = hgat[2]
        hgat[1] = hgat[2]
        og_all = ogat[...].reshape(32 * nt, 128)
        og_two = jnp.concatenate([og_all, move_in_16(og_all.astype(F32), 1).astype(BF16)], axis=1)
        for a in range(3):
            for b in range(3):
                for p in range(2):
                    lhs = jnp.concatenate(
                        [
                            hgat[2 * f + a, 2 * r + b, 16 * p : 16 * p + 16]
                            for f in range(nt)
                            for r in range(2)
                        ],
                        axis=0,
                    )
                    q = lax.dot_general(
                        lhs, og_all if p else og_two, TN, preferred_element_type=F32
                    )
                    n = 128 * (a * 9 + b * 3)
                    if p:
                        part[n + 128 : n + 256] = q
                    else:
                        part[n : n + 128] = q[:, :128]
                        part[n + 256 : n + 384] = q[:, 128:]

    half = chip // 2

    def cut(k, carry):
        start = (groups * k + 1 - half) // 2
        rows = part[pl.ds(pl.multiple_of(start * 8, 8), slot)]
        sl[k % ny, k // ny] = rows.astype(BF16)
        return carry

    lax.fori_loop(0, ny * nz, cut, 0)
    y_sends = []
    for k in range(1, ny):
        to = (y + k) % ny
        y_sends.append(send(sl.at[to], r1.at[k - 1], rs1s.at[k - 1], rs1r.at[k - 1], at_y(to)))
    for c in y_sends:
        c.start()

    for c in g_halo:
        c.wait_recv()

    @pl.when(t == nt - 1)
    def _():
        ge[2:4] = jnp.zeros((2, 6, 32, 256), BF16)

    @pl.when(h == 0)
    def _():
        ge[:, 0] = jnp.zeros((4, 32, 256), BF16)

    @pl.when(h == nh - 1)
    def _():
        ge[:, 5] = jnp.zeros((4, 32, 256), BF16)

    sums = [None] * 3
    for a in range(3):
        for b in range(3):
            lhs = ge[2 - a : 4 - a, 2 - b : 6 - b].reshape(256, 256)
            for e in range(3):
                q = lax.dot_general(lhs, w1[a * 9 + b * 3 + e], NT, preferred_element_type=F32)
                sums[e] = q if sums[e] is None else sums[e] + q
    for e in range(3):
        zs[e] = sums[e]

    @pl.when(first)
    def _():
        for e in range(3):
            total = zs[e, 0:128]
            for a, f in ((0, 0), (0, 1), (1, 0)):
                for b in range(3):
                    lhs = ge[f, 2 - b : 6 - b].reshape(128, 256)
                    total = total + lax.dot_general(
                        lhs, w1[a * 9 + b * 3 + e], NT, preferred_element_type=F32
                    )
            zs[e, 0:128] = total

    clip = (from_right(zs[0]) + zs[1] + from_left(zs[2])).astype(BF16)
    clip_ref[...] = lax.dot_general(
        column_order(256), clip, TN, preferred_element_type=F32
    ).astype(BF16)

    for c in y_sends:
        c.wait_recv()

    def add_y(k, carry):
        total = sl[y, k].astype(F32)
        for n in range(ny - 1):
            total = total + r1[n, k].astype(F32)
        s1[k] = total.astype(BF16)
        return carry

    lax.fori_loop(0, nz, add_y, 0)
    z_sends = []
    for k in range(1, nz):
        to = (z + k) % nz
        where = (t, to * 2 + h % 2, d)
        z_sends.append(send(s1.at[to], r2.at[k - 1], rs2s.at[k - 1], rs2r.at[k - 1], where))
    for c in z_sends:
        c.start()
    total = s1[z].astype(F32)
    for k, c in enumerate(z_sends):
        c.wait_recv()
        total = total + r2[k].astype(F32)
    fs[...] = total.astype(BF16)
    t_sends = []
    for k in range(1, nt):
        where = ((t + k) % nt, h, d)
        t_sends.append(send(fs, fg.at[t], ags.at[k - 1], agr.at[k - 1], where))
    for c in t_sends:
        c.start()
    fg[t] = fs[...]
    for k in range(1, nt):
        s = (t + nt - k) % nt
        send(fs, fg.at[s], ags.at[k - 1], agr.at[k - 1], (s, h, d)).wait_recv()

    cells = sizes[0] * sizes[1] * sizes[2] * 256
    scale = (1.0 / math.sqrt(cells), 1.0 / math.sqrt(cells // 8))
    for s in range(nt):
        ff[s] = fg[s].astype(F32) * scale[s % 2]
    for j in range(groups):
        parity = (groups * block + j) % 2
        for o in range(2):
            for k, out in enumerate((conv_ref, down_ref)):
                source = 2 * (2 * parity + o) + k
                out[8 * j : 8 * j + 8, 128 * o : 128 * o + 128] = ff[
                    source, 8 * (j // 2) : 8 * (j // 2) + 8
                ]

    for c in og_halo + x_halo + [h_rows] + h_halo + g_halo + y_sends + z_sends + t_sends:
        c.wait_send()
    gather_sent(1, *og_move)
    gather_sent(0, *x_move)
    gather_sent(0, *g_move)
    gather_sent(1, *h_move)


def body(mesh_sizes, video_clip, conv_weight, down_weight, output_grad):
    nt, nh, nd = mesh_sizes
    ny, nz = 2 * nd, nh // 2
    blocks = ny * nz
    groups = 864 // blocks
    slot = 8 * ((groups + 1) // 2)
    dma = pltpu.SemaphoreType.DMA

    def vm(*shape, dtype=BF16):
        return pltpu.VMEM(shape, dtype)

    scratch = [
        vm(27, 256, 256), vm(27, 256, 256),
        vm(4, 6, 32, 256), vm(2, 3, 16, 256), vm(4, 5, 32, 256), vm(4, 6, 32, 256),
        vm(2, 4, 32, 256, dtype=F32), vm(256, 256, dtype=F32), vm(3, 256, 256, dtype=F32),
        vm(2, 2, 6, 32, 128), vm(2, 2, 4, 32, 128), vm(2, 2, 5, 32, 128), vm(2, 2, 16, 128),
        vm(2 * nt + 2, 6, 32, 128), vm(2 * nt, 4, 32, 128),
        vm(2 * nt + 2, 5, 32, 128), vm(nt, 2, 16, 128),
        vm(2 * nt + 2, 384, 128), vm(256 * nt, 384), vm(27 * 128 + 8, 128, dtype=F32),
        vm(ny, nz, slot, 128), vm(ny - 1, nz, slot, 128),
        vm(nz, slot, 128), vm(nz - 1, slot, 128),
        vm(slot, 128), vm(nt, slot, 128), vm(nt, slot, 128, dtype=F32),
        dma((2,)), dma((8,)), dma((8,)), dma((8,)), dma((8,)),
    ]
    scratch += [dma((n,)) for _ in range(4) for n in (nt // 2, nt)]
    scratch += [dma((n,)) for n in (ny - 1, ny - 1, nz - 1, nz - 1, nt - 1, nt - 1)]
    vmem = pl.BlockSpec(memory_space=pltpu.VMEM)
    hbm = pl.BlockSpec(memory_space=pl.ANY)
    enc, clip, conv, down = pl.pallas_call(
        functools.partial(kernel, mesh_sizes),
        out_shape=(
            jax.ShapeDtypeStruct((32, 256), BF16),
            jax.ShapeDtypeStruct((256, 256), BF16),
            jax.ShapeDtypeStruct((groups * 8, 256), F32),
            jax.ShapeDtypeStruct((groups * 8, 256), F32),
        ),
        in_specs=[vmem, hbm, hbm, vmem],
        out_specs=(vmem,) * 4,
        scratch_shapes=scratch,
        compiler_params=pltpu.CompilerParams(
            collective_id=0, has_side_effects=True, vmem_limit_bytes=44 * 2**20
        ),
    )(
        video_clip.reshape(256, 256),
        conv_weight.reshape(27, 256, 256),
        down_weight.reshape(27, 256, 256),
        output_grad.reshape(32, 256),
    )
    return enc.reshape(1, 1, 2, 16, 256), clip.reshape(1, 2, 4, 32, 256), conv, down


def solution(mesh):
    sizes = tuple(mesh.shape[a] for a in ("tm", "height", "dp"))
    cells = P("dp", "tm", "height", None, None)
    rows = P(("height", "dp"), None)
    return jax.shard_map(
        functools.partial(body, sizes),
        mesh=mesh,
        in_specs=(cells, P(), P(), cells),
        out_specs=(cells, cells, rows, rows),
        check_vma=False,
    )
```

```python
import functools
import math

import jax
import jax.numpy as jnp
from jax import lax
from jax.experimental import pallas as pl
from jax.experimental.pallas import tpu as pltpu
from jax.sharding import PartitionSpec as P

MESH = pl.DeviceIdType.MESH
F32 = jnp.float32
BF16 = jnp.bfloat16
NT = (((1,), (1,)), ((), ()))
TN = (((0,), (0,)), ((), ()))


def iota2(shape, dim):
    return lax.broadcasted_iota(jnp.int32, shape, dim)


def one_hot(mask):
    return jnp.where(mask, 1.0, 0.0).astype(F32).astype(BF16)


def column_order(n):
    m, k = iota2((n, n), 0), iota2((n, n), 1)
    return one_hot(k == (m & ~31) + 2 * (m & 15) + ((m >> 4) & 1))


def channel_order(n):
    i, k = iota2((n, n), 0), iota2((n, n), 1)
    j = k & 127
    return one_hot(i == (j >> 3) * 16 + (k >> 7) * 8 + (j & 7))


def quarter_order(n):
    i, k = iota2((2 * n, 2 * n), 0), iota2((2 * n, 2 * n), 1)
    j = k & 63
    return one_hot(i == ((k >> 6) & 1) * n + (j >> 3) * 32 + (k >> 7) * 8 + (j & 7))


def move_in_16(x, step):
    n = x.shape[0]
    k = iota2(x.shape, 0) & 15
    rolled = pltpu.roll(x, step % n, 0)
    return jnp.where(k == (0 if step == 1 else 15), 0.0, rolled)


def halves(x):
    groups = x.shape[0] // 32
    parts = x.reshape(groups, 2, 16, x.shape[1])
    return parts[:, 0].reshape(groups * 16, -1), parts[:, 1].reshape(groups * 16, -1)


def joined(even, odd):
    groups = even.shape[0] // 16
    parts = [h.reshape(groups, 1, 16, h.shape[1]) for h in (even, odd)]
    return jnp.concatenate(parts, axis=1).reshape(groups * 32, -1)


def from_left(x):
    even, odd = halves(x)
    return joined(move_in_16(odd, 1), even)


def from_right(x):
    even, odd = halves(x)
    return joined(odd, move_in_16(even, -1))


def kernel(
    sizes,
    x_hbm, w1_hbm, w2_hbm, og_hbm,
    enc_ref, clip_ref, fg,
    x_ref, og_ref, w1, w2, xe, oge, he, ge, hg, zs,
    xs, xsh, gs, hs, hsh, xg, xgh, gg, hgat, hgh, ogat, xt, g3, part, part4,
    sl, r1, s1, r2, fs,
    wsem, p1s, p1r, p2s, p2r,
    xss, xsr, xhs, xhr, gss, gsr, hss, hsr, hhs, hhr, oss, osr,
    rs1s, rs1r, rs2s, rs2r, ags, agr,
):
    nt, nh, nd = sizes
    ny, nz = 2 * nd, nh // 2
    t, h, d = lax.axis_index("tm"), lax.axis_index("height"), lax.axis_index("dp")
    y, z = (h % 2) * nd + d, h // 2
    core, chip = t % 2, t // 2
    t_next, t_prev = (t + 1) % nt, (t + nt - 1) % nt
    h_next, h_prev = (h + 1) % nh, (h + nh - 1) % nh
    block = z * ny + y
    groups = 864 // (ny * nz)
    slot = 8 * ((groups + 1) // 2)

    wc1 = pltpu.make_async_copy(w1_hbm, w1, wsem.at[0])
    wc2 = pltpu.make_async_copy(w2_hbm, w2, wsem.at[1])
    og_in = pltpu.make_async_copy(og_hbm, og_ref, wsem.at[2])
    x_in = pltpu.make_async_copy(x_hbm, x_ref, wsem.at[3])
    for c in (og_in, x_in, wc2, wc1):
        c.start()

    def at_y(k):
        return (t, z * 2 + k // nd, k % nd)

    barrier = pltpu.get_barrier_semaphore()

    def greet(where):
        pl.semaphore_signal(barrier, inc=1, device_id=where, device_id_type=MESH)

    for k in range(1, nt):
        greet(((t + k) % nt, h, d))
    for hh in (h_next, h_prev):
        for tt in (t_prev, t, t_next):
            greet((tt, hh, d))
    for k in range(1, ny):
        greet(at_y((y + k) % ny))
    for k in range(1, nz):
        greet((t, ((z + k) % nz) * 2 + h % 2, d))

    og_in.wait()
    x_in.wait()
    x_own = jnp.dot(column_order(256), x_ref[...], preferred_element_type=F32).astype(BF16)
    xe[2:4, 1:5] = x_own.reshape(2, 4, 32, 256)
    oge[0, 1:3] = og_ref[...].reshape(2, 16, 256)
    by_channel = channel_order(256)

    def keep_halves(block, out, rows):
        moved = jnp.dot(block, by_channel, preferred_element_type=F32).astype(BF16)
        for k in range(2):
            out[k] = moved[:, 128 * k : 128 * (k + 1)].reshape(2, rows, 32, 128)

    keep_halves(x_own, xs, 4)

    pl.semaphore_wait(barrier, (nt - 1) + 6 + (ny - 1) + (nz - 1))

    def send(src, dst, ssem, rsem, where):
        return pltpu.make_async_remote_copy(
            src_ref=src, dst_ref=dst, send_sem=ssem, recv_sem=rsem, device_id=where, device_id_type=MESH
        )

    def p1(k, src, dst, where):
        return send(src, dst, p1s.at[k], p1r.at[k], where)

    og_halo = [
        p1(0, oge.at[0:1, 1:3], oge.at[1:2, 1:3], (t_prev, h, d)),
        p1(1, oge.at[0:1, 2:3], oge.at[0:1, 0:1], (t, h_next, d)),
        p1(2, oge.at[0:1, 2:3], oge.at[1:2, 0:1], (t_prev, h_next, d)),
    ]
    x_halo = [
        p1(3, xe.at[2:4, 1:5], xe.at[0:2, 1:5], (t_next, h, d)),
        p1(4, xe.at[2:4, 4:5], xe.at[2:4, 0:1], (t, h_next, d)),
        p1(5, xe.at[2:4, 1:2], xe.at[2:4, 5:6], (t, h_prev, d)),
        p1(6, xe.at[2:4, 4:5], xe.at[0:2, 0:1], (t_next, h_next, d)),
        p1(7, xe.at[2:4, 1:2], xe.at[0:2, 5:6], (t_next, h_prev, d)),
    ]
    for c in og_halo + x_halo:
        c.start()

    def gather_sends(role, source, target, ssem, rsem):
        for k in range(nt // 2):
            to_chip = (chip + k) % (nt // 2)
            to = to_chip * 2 + role
            c = send(source(to_chip), target(t), ssem.at[k], rsem.at[t], (to, h, d))
            if k == 0:
                pl.when(core != role)(c.start)
            else:
                c.start()

    def gather_sent(role, source, target, ssem, rsem):
        for k in range(nt // 2):
            to_chip = (chip + k) % (nt // 2)
            c = send(source(to_chip), target(t), ssem.at[k], rsem.at[t], (to_chip * 2 + role, h, d))
            if k == 0:
                pl.when(core != role)(c.wait_send)
            else:
                c.wait_send()

    def gather_received(source, target, ssem, rsem):
        for k in range(1, nt):
            s = (t + k) % nt
            send(source(0), target(s), ssem.at[0], rsem.at[s], (s, h, d)).wait_recv()

    def later_frames(ref):
        return lambda s: ref.at[pl.ds(2 + 2 * s, 2)]

    og_move = (lambda c: oge.at[0, 1:3], lambda s: ogat.at[s], oss, osr)
    x_move = (lambda c: xs.at[c // 2], later_frames(xg), xss, xsr)
    x_rim_move = (lambda c: xsh.at[c // 2], later_frames(xgh), xhs, xhr)
    g_move = (lambda c: gs.at[c % 2], lambda s: gg.at[pl.ds(2 * s, 2)], gss, gsr)
    h_move = (lambda c: hs.at[c], later_frames(hgat), hss, hsr)
    h_rim_move = (lambda c: hsh.at[c], later_frames(hgh), hhs, hhr)
    gather_sends(1, *og_move)

    wc2.wait()
    for c in og_halo:
        c.wait_recv()
    gather_sends(0, *x_move)

    @pl.when(t == nt - 1)
    def _():
        oge[1] = jnp.zeros((3, 16, 256), BF16)

    @pl.when(h == 0)
    def _():
        oge[:, 0] = jnp.zeros((2, 16, 256), BF16)

    og_rows = oge[...].reshape(96, 256)
    first = t == 0
    terms = {}
    for e in range(3):
        for a in range(3):
            for b in range(3):
                lhs = og_rows if a < 2 else og_rows[:48]
                q = lax.dot_general(lhs, w2[a * 9 + b * 3 + e], NT, preferred_element_type=F32)
                offset = 0 if b == 2 else 16
                here = q[offset : offset + 32]
                if a < 2:
                    here = jnp.where(first, here, 0.0)
                    later = q[48 + offset : 48 + offset + 32]
                    key = (a, b % 2, e)
                    terms[key] = terms.get(key, 0.0) + later
                key = (0, b % 2, e)
                terms[key] = terms.get(key, 0.0) + here
    for f in range(2):
        for b in range(2):
            even = terms[f, b, 0] + move_in_16(terms[f, b, 2], 1)
            odd = terms[f, b, 1]
            for u in range(2):
                hg[f, 2 * u + b, 0:16] = even[16 * u : 16 * u + 16]
                hg[f, 2 * u + b, 16:32] = odd[16 * u : 16 * u + 16]

    for c in x_halo:
        c.wait_recv()

    @pl.when(h == 0)
    def _():
        xe[:, 0] = jnp.zeros((4, 32, 256), BF16)

    @pl.when(h == nh - 1)
    def _():
        xe[:, 5] = jnp.zeros((4, 32, 256), BF16)

    @pl.when(first)
    def _():
        xe[0] = xe[2]
        xe[1] = xe[2]

    rims = jnp.concatenate([xe[2:4, 0:1], xe[2:4, 5:6]], axis=1)
    keep_halves(rims.reshape(128, 256), xsh, 2)
    gather_sends(0, *x_rim_move)

    wc1.wait()
    sums = [None] * 3
    for a in range(3):
        for b in range(3):
            lhs = xe[a : a + 2, b : b + 4].reshape(256, 256)
            for e in range(3):
                q = jnp.dot(lhs, w1[a * 9 + b * 3 + e], preferred_element_type=F32)
                sums[e] = q if sums[e] is None else sums[e] + q
    value = from_left(sums[0]) + sums[1] + from_right(sums[2])
    sigmoid = jax.nn.sigmoid(value)
    he[2:4, 0:4] = (value * sigmoid).astype(BF16).reshape(2, 4, 32, 256)
    slope = sigmoid * (1.0 + value * (1.0 - sigmoid))
    grad = (hg[...].reshape(256, 256) * slope).astype(BF16)
    ge[0:2, 1:5] = grad.reshape(2, 4, 32, 256)
    for k in range(2):
        gs[k] = grad[:, 128 * k : 128 * (k + 1)].reshape(2, 4, 32, 128)

    def p2(k, src, dst, where):
        return send(src, dst, p2s.at[k], p2r.at[k], where)

    h_rows = p2(0, he.at[2:4, 0:1], he.at[2:4, 4:5], (t, h_prev, d))
    g_rows = [
        p2(1, ge.at[0:2, 4:5], ge.at[0:2, 0:1], (t, h_next, d)),
        p2(2, ge.at[0:2, 1:2], ge.at[0:2, 5:6], (t, h_prev, d)),
    ]
    h_frames = p2(3, he.at[2:4], he.at[0:2], (t_next, h, d))
    g_frames = p2(4, ge.at[0:2], ge.at[2:4], (t_prev, h, d))
    h_rows.start()
    gather_sends(0, *g_move)
    by_quarter = quarter_order(256)

    def keep_quarters(block, out, rows):
        lanes = [block[..., p : p + 16, :].reshape(32 * rows, 256) for p in (0, 16)]
        both = jnp.concatenate(lanes, axis=1)
        moved = jnp.dot(both, by_quarter, preferred_element_type=F32).astype(BF16)
        for k in range(4):
            out[k] = moved[:, 128 * k : 128 * (k + 1)].reshape(2, rows, 16, 128)

    keep_quarters(he[2:4, 0:4], hs, 4)
    gather_sends(1, *h_move)
    for c in g_rows:
        c.start()
    h_rows.wait_recv()

    @pl.when(h == nh - 1)
    def _():
        he[2:4, 4] = jnp.zeros((2, 32, 256), BF16)

    keep_quarters(he[2:4, 4:5], hsh, 1)
    gather_sends(1, *h_rim_move)
    for c in g_rows:
        c.wait_recv()

    @pl.when(h == 0)
    def _():
        ge[0:2, 0] = jnp.zeros((2, 32, 256), BF16)

    @pl.when(h == nh - 1)
    def _():
        ge[0:2, 5] = jnp.zeros((2, 32, 256), BF16)

    @pl.when(core == 0)
    def _():
        part[pl.ds(27 * 128, 8)] = jnp.zeros((8, 128), F32)
        xg[pl.ds(2 + 2 * t, 2)] = xs[chip // 2]
        xgh[pl.ds(2 + 2 * t, 2)] = xsh[chip // 2]
        gg[pl.ds(2 * t, 2)] = gs[chip % 2]
        gather_received(*x_move)
        gather_received(*x_rim_move)
        for f in range(2):
            xg[f] = xg[2]
            xgh[f] = xgh[2]

        def turn(f, carry):
            rows = jnp.concatenate([xgh[f, 0:1], xg[f], xgh[f, 1:2]], axis=0)
            for b in range(3):
                xt[f, 128 * b : 128 * (b + 1)] = rows[b : b + 4].reshape(128, 128).T
            return carry

        lax.fori_loop(0, 2 * nt + 2, turn, 0)
        gather_received(*g_move)

        def spread(s, carry):
            rows = pl.ds(pl.multiple_of(256 * s, 256), 256)
            g = gg[pl.ds(2 * s, 2)].reshape(256, 128)
            wide = g.astype(F32)
            g3[rows, 0:128] = from_right(wide).astype(BF16)
            g3[rows, 128:256] = g
            g3[rows, 256:384] = from_left(wide).astype(BF16)
            return carry

        lax.fori_loop(0, nt, spread, 0)

    @pl.when(core == 1)
    def _():
        part4[pl.ds(27 * 64, 8)] = jnp.zeros((8, 256), F32)
        hgat[pl.ds(2 + 2 * t, 2)] = hs[chip]
        hgh[pl.ds(2 + 2 * t, 2)] = hsh[chip]
        ogat[t] = oge[0, 1:3]
        gather_received(*og_move)
        og_all = ogat[...].reshape(32 * nt, 256)
        og_two = jnp.concatenate([og_all, move_in_16(og_all.astype(F32), 1).astype(BF16)], axis=1)
        gather_received(*h_move)
        gather_received(*h_rim_move)
        for f in range(2):
            hgat[f] = hgat[2]
            hgh[f] = hgh[2]
        for a in range(3):
            for b in range(3):
                pieces = [
                    hgh[2 * f + a, 0] if b + 2 * r == 4 else hgat[2 * f + a, b + 2 * r]
                    for f in range(nt)
                    for r in range(2)
                ]
                lhs = jnp.concatenate(pieces, axis=0)
                q = lax.dot_general(lhs, og_two, TN, preferred_element_type=F32)
                n = 64 * (a * 9 + b * 3)
                part4[n : n + 64] = q[0:64, 0:256]
                part4[n + 64 : n + 128] = q[64:128, 0:256]
                part4[n + 128 : n + 192] = q[0:64, 256:512]

    h_frames.start()
    g_frames.start()

    pair = nz // 3 if nz == 8 else 0

    def chunk_at(j):
        if j < 3 * pair:
            return 3 * ((z + j // pair) % 3) + j % pair
        return (2, 5)[j - 3 * pair] if pair else (z + 1 + j) % nz

    def y_copies(j):
        c = chunk_at(j)
        return [
            send(
                sl.at[(y + k) % ny, c], r1.at[k - 1, c],
                rs1s.at[j, k - 1], rs1r.at[j, k - 1], at_y((y + k) % ny),
            )
            for k in range(1, ny)
        ]

    def send_chunk(j):
        c = chunk_at(j)

        def cut(k, carry):
            n = groups * (c * ny + k)

            @pl.when(core == 0)
            def _():
                first_row = pl.multiple_of((n + 1 - chip // 2) // 2 * 8, 8)
                sl[k, c] = part[pl.ds(first_row, slot)].astype(BF16)

            @pl.when(core == 1)
            def _():
                first_row = pl.multiple_of((n + 3 - chip) // 4 * 8, 8)
                rows = part4[pl.ds(first_row, slot // 2)]
                stacked = jnp.concatenate([rows[:, :128], rows[:, 128:]], axis=0)
                sl[k, c] = stacked.astype(BF16)

            return carry

        lax.fori_loop(0, ny, cut, 0)
        for copy in y_copies(j):
            copy.start()

    for k in range(3):

        @pl.when(core == 0)
        def _():
            a = (z + k) % 3
            lhs = jnp.concatenate([xt[a + f] for f in range(2 * nt)], axis=1)
            q = jnp.dot(lhs, g3[...], preferred_element_type=F32)
            for b in range(3):
                for e in range(3):
                    n = pl.multiple_of(128 * (a * 9 + b * 3 + e), 128)
                    part[pl.ds(n, 128)] = q[128 * b : 128 * (b + 1), 128 * e : 128 * (e + 1)]

        for j in range(k * pair, (k + 1) * pair):
            send_chunk(j)
    for j in range(3 * pair, nz):
        send_chunk(j)

    def z_copy(j):
        c = chunk_at(j)
        step = (c - z + nz) % nz
        k = jnp.maximum(step - 1, 0)
        where = (t, c * 2 + h % 2, d)
        return step, send(s1.at[c], r2.at[k], rs2s.at[k], rs2r.at[k], where)

    def pass_chunk(j):
        c = chunk_at(j)
        for copy in y_copies(j):
            copy.wait_recv()
        total = sl[y, c].astype(F32)
        for n in range(ny - 1):
            total = total + r1[n, c].astype(F32)
        s1[c] = total.astype(BF16)
        step, copy = z_copy(j)
        pl.when(step > 0)(copy.start)

    for j in range(nz // 4):
        pass_chunk(j)

    h_frames.wait_recv()

    @pl.when(first)
    def _():
        he[0] = he[2]
        he[1] = he[2]

    sums = [None] * 3
    for a in range(3):
        for b in range(3):
            for e in range(3):
                p = 16 * (e % 2)
                lhs = jnp.concatenate([he[a, b, p : p + 16], he[a, b + 2, p : p + 16]], axis=0)
                q = jnp.dot(lhs, w2[a * 9 + b * 3 + e], preferred_element_type=F32)
                sums[e] = q if sums[e] is None else sums[e] + q
    enc_ref[...] = (sums[0] + sums[1] + move_in_16(sums[2], -1)).astype(BF16)
    for j in range(nz // 4, nz // 2):
        pass_chunk(j)

    g_frames.wait_recv()

    @pl.when(t == nt - 1)
    def _():
        ge[2:4] = jnp.zeros((2, 6, 32, 256), BF16)

    sums = [None] * 3
    for a in range(3):
        for b in range(3):
            lhs = ge[2 - a : 4 - a, 2 - b : 6 - b].reshape(256, 256)
            for e in range(3):
                q = lax.dot_general(lhs, w1[a * 9 + b * 3 + e], NT, preferred_element_type=F32)
                sums[e] = q if sums[e] is None else sums[e] + q
    for e in range(3):
        zs[e] = sums[e]

    for j in range(nz // 2, 3 * nz // 4):
        pass_chunk(j)

    @pl.when(first)
    def _():
        for e in range(3):
            total = zs[e, 0:128]
            for a, f in ((0, 0), (0, 1), (1, 0)):
                for b in range(3):
                    lhs = ge[f, 2 - b : 6 - b].reshape(128, 256)
                    total = total + lax.dot_general(
                        lhs, w1[a * 9 + b * 3 + e], NT, preferred_element_type=F32
                    )
            zs[e, 0:128] = total

    clip = (from_right(zs[0]) + zs[1] + from_left(zs[2])).astype(BF16)
    clip_ref[...] = lax.dot_general(
        column_order(256), clip, TN, preferred_element_type=F32
    ).astype(BF16)

    for j in range(3 * nz // 4, nz):
        pass_chunk(j)
    total = s1[z].astype(F32)
    for k in range(1, nz):
        source = ((z - k + nz) % nz * 2 + h % 2, d)
        send(
            s1.at[z], r2.at[k - 1], rs2s.at[k - 1], rs2r.at[k - 1], (t, *source)
        ).wait_recv()
        total = total + r2[k - 1].astype(F32)
    fs[...] = total.astype(BF16)
    t_sends = []
    for k in range(1, nt):
        where = ((t + k) % nt, h, d)
        t_sends.append(send(fs, fg.at[t], ags.at[k - 1], agr.at[k - 1], where))
    for c in t_sends:
        c.start()
    fg[t] = fs[...]
    for k in range(1, nt):
        s = (t + nt - k) % nt
        send(fs, fg.at[s], ags.at[k - 1], agr.at[k - 1], (s, h, d)).wait_recv()

    for c in og_halo + x_halo + [h_rows] + g_rows + [h_frames, g_frames] + t_sends:
        c.wait_send()
    for j in range(nz):
        for copy in y_copies(j):
            copy.wait_send()
        step, copy = z_copy(j)
        pl.when(step > 0)(copy.wait_send)
    for move in (x_move, x_rim_move, g_move):
        gather_sent(0, *move)
    for move in (og_move, h_move, h_rim_move):
        gather_sent(1, *move)


def finish(sizes, enc_ref, clip_ref, fg, enc_hbm, clip_hbm, conv_hbm, down_hbm, ff, conv, down, sem):
    nt, nh, nd = sizes
    block = lax.axis_index("height") * nd + lax.axis_index("dp")
    groups = 864 // (nh * nd)
    slot = fg.shape[1]
    early = [
        pltpu.make_async_copy(enc_ref, enc_hbm, sem.at[0]),
        pltpu.make_async_copy(clip_ref, clip_hbm, sem.at[1]),
    ]
    for c in early:
        c.start()
    cells = nt * nh * nd * 256
    scale = (1.0 / math.sqrt(cells), 1.0 / math.sqrt(cells // 8))
    for s in range(nt):
        ff[s] = fg[s].astype(F32) * scale[s % 2]
    late = []
    for k, (out, hbm) in enumerate(((conv, conv_hbm), (down, down_hbm))):
        for j in range(groups):
            n = groups * block + j
            for o in range(2):
                if k == 0:
                    rows = ff[2 * (2 * (n % 2) + o), 8 * (j // 2) : 8 * (j // 2) + 8]
                else:
                    row = o * (slot // 2) + 8 * (j // 4)
                    rows = ff[2 * (n % 4) + 1, row : row + 8]
                out[8 * j : 8 * j + 8, 128 * o : 128 * o + 128] = rows
        c = pltpu.make_async_copy(out, hbm, sem.at[2 + k])
        c.start()
        late.append(c)
    for c in early + late:
        c.wait()


def body(mesh_sizes, video_clip, conv_weight, down_weight, output_grad):
    nt, nh, nd = mesh_sizes
    ny, nz = 2 * nd, nh // 2
    blocks = ny * nz
    groups = 864 // blocks
    slot = 8 * ((groups + 1) // 2)
    dma = pltpu.SemaphoreType.DMA

    def vm(*shape, dtype=BF16):
        return pltpu.VMEM(shape, dtype)

    scratch = [
        vm(256, 256), vm(32, 256), vm(27, 256, 256), vm(27, 256, 256),
        vm(4, 6, 32, 256), vm(2, 3, 16, 256), vm(4, 5, 32, 256), vm(4, 6, 32, 256),
        vm(2, 4, 32, 256, dtype=F32), vm(3, 256, 256, dtype=F32),
        vm(2, 2, 4, 32, 128), vm(2, 2, 2, 32, 128), vm(2, 2, 4, 32, 128),
        vm(4, 2, 4, 16, 128), vm(4, 2, 1, 16, 128),
        vm(2 * nt + 2, 4, 32, 128), vm(2 * nt + 2, 2, 32, 128), vm(2 * nt, 4, 32, 128),
        vm(2 * nt + 2, 4, 16, 128), vm(2 * nt + 2, 1, 16, 128), vm(nt, 2, 16, 256),
        vm(2 * nt + 2, 384, 128), vm(256 * nt, 384),
        vm(27 * 128 + 8, 128, dtype=F32), vm(27 * 64 + 8, 256, dtype=F32),
        vm(ny, nz, slot, 128), vm(ny - 1, nz, slot, 128),
        vm(nz, slot, 128), vm(nz - 1, slot, 128),
        vm(slot, 128),
        dma((4,)), dma((8,)), dma((8,)), dma((5,)), dma((5,)),
    ]
    scratch += [dma((n,)) for _ in range(6) for n in (nt // 2, nt)]
    scratch += [dma(n) for n in ((nz, ny - 1),) * 2 + ((nz - 1,),) * 2 + ((nt - 1,),) * 2]
    vmem = pl.BlockSpec(memory_space=pltpu.VMEM)
    hbm = pl.BlockSpec(memory_space=pltpu.HBM)
    shape = jax.ShapeDtypeStruct
    features = (shape((32, 256), BF16), shape((256, 256), BF16))
    gathered = pl.pallas_call(
        functools.partial(kernel, mesh_sizes),
        out_shape=(*features, shape((nt, slot, 128), BF16)),
        in_specs=[hbm] * 4,
        out_specs=(vmem,) * 3,
        scratch_shapes=scratch,
        compiler_params=pltpu.CompilerParams(
            collective_id=0, has_side_effects=True, vmem_limit_bytes=44 * 2**20
        ),
    )(
        *(
            pltpu.with_memory_space_constraint(operand, pltpu.HBM)
            for operand in (
                video_clip.reshape(256, 256),
                conv_weight.reshape(27, 256, 256),
                down_weight.reshape(27, 256, 256),
                output_grad.reshape(32, 256),
            )
        )
    )
    rows = shape((groups * 8, 256), F32)
    enc, clip, conv, down = pl.pallas_call(
        functools.partial(finish, mesh_sizes),
        out_shape=(*features, rows, rows),
        in_specs=[vmem] * 3,
        out_specs=(hbm,) * 4,
        scratch_shapes=[
            vm(nt, slot, 128, dtype=F32),
            vm(groups * 8, 256, dtype=F32),
            vm(groups * 8, 256, dtype=F32),
            dma((4,)),
        ],
        compiler_params=pltpu.CompilerParams(vmem_limit_bytes=16 * 2**20),
    )(*gathered)
    return enc.reshape(1, 1, 2, 16, 256), clip.reshape(1, 2, 4, 32, 256), conv, down


def solution(mesh):
    sizes = tuple(mesh.shape[a] for a in ("tm", "height", "dp"))
    cells = P("dp", "tm", "height", None, None)
    rows = P(("height", "dp"), None)
    return jax.shard_map(
        functools.partial(body, sizes),
        mesh=mesh,
        in_specs=(cells, P(), P(), cells),
        out_specs=(cells, cells, rows, rows),
        check_vma=False,
    )
```

```python
import functools
import math

import jax
import jax.numpy as jnp
from jax import lax
from jax.experimental import pallas as pl
from jax.experimental.pallas import tpu as pltpu
from jax.sharding import PartitionSpec as P

MESH = pl.DeviceIdType.MESH
F32 = jnp.float32
BF16 = jnp.bfloat16
NT = (((1,), (1,)), ((), ()))
TN = (((0,), (0,)), ((), ()))


def iota2(shape, dim):
    return lax.broadcasted_iota(jnp.int32, shape, dim)


def one_hot(mask):
    return jnp.where(mask, 1.0, 0.0).astype(F32).astype(BF16)


def column_order(n):
    m, k = iota2((n, n), 0), iota2((n, n), 1)
    return one_hot(k == (m & ~31) + 2 * (m & 15) + ((m >> 4) & 1))


def channel_order(n):
    i, k = iota2((n, n), 0), iota2((n, n), 1)
    j = k & 127
    return one_hot(i == (j >> 3) * 16 + (k >> 7) * 8 + (j & 7))


def quarter_order(n):
    i, k = iota2((2 * n, 2 * n), 0), iota2((2 * n, 2 * n), 1)
    j = k & 63
    return one_hot(i == ((k >> 6) & 1) * n + (j >> 3) * 32 + (k >> 7) * 8 + (j & 7))


def move_in_16(x, step):
    n = x.shape[0]
    k = iota2(x.shape, 0) & 15
    rolled = pltpu.roll(x, step % n, 0)
    return jnp.where(k == (0 if step == 1 else 15), 0.0, rolled)


def halves(x):
    groups = x.shape[0] // 32
    parts = x.reshape(groups, 2, 16, x.shape[1])
    return parts[:, 0].reshape(groups * 16, -1), parts[:, 1].reshape(groups * 16, -1)


def joined(even, odd):
    groups = even.shape[0] // 16
    parts = [h.reshape(groups, 1, 16, h.shape[1]) for h in (even, odd)]
    return jnp.concatenate(parts, axis=1).reshape(groups * 32, -1)


def from_left(x):
    even, odd = halves(x)
    return joined(move_in_16(odd, 1), even)


def from_right(x):
    even, odd = halves(x)
    return joined(odd, move_in_16(even, -1))


def kernel(
    sizes,
    x_hbm, w1_hbm, w2_hbm, og_hbm,
    enc_ref, clip_ref, fg,
    by_column, by_channel, by_quarter, x_ref, og_ref, w1, w2, xe, oge, he, ge, hg, zs,
    xs, xsh, gs, hs, hsh, xg, xgh, gg, hgat, hgh, ogat, xt, g3, part, part4,
    sl, r1, s1, r2, fs,
    wsem, p1s, p1r, p2s, p2r,
    xss, xsr, xhs, xhr, gss, gsr, hss, hsr, hhs, hhr, oss, osr,
    rs1s, rs1r, rs2s, rs2r, ags, agr,
):
    nt, nh, nd = sizes
    ny, nz = 2 * nd, nh // 2
    t, h, d = lax.axis_index("tm"), lax.axis_index("height"), lax.axis_index("dp")
    y, z = (h % 2) * nd + d, h // 2
    core, chip = t % 2, t // 2
    t_next, t_prev = (t + 1) % nt, (t + nt - 1) % nt
    h_next, h_prev = (h + 1) % nh, (h + nh - 1) % nh
    block = z * ny + y
    groups = 864 // (ny * nz)
    slot = 8 * ((groups + 1) // 2)

    wc1 = pltpu.make_async_copy(w1_hbm, w1, wsem.at[0])
    wc2 = pltpu.make_async_copy(w2_hbm, w2, wsem.at[1])
    first = t == 0
    og_in = pltpu.make_async_copy(og_hbm, og_ref, wsem.at[2])
    x_in = pltpu.make_async_copy(x_hbm, x_ref, wsem.at[3])
    for c in (x_in, og_in, wc1, wc2):
        c.start()

    def at_y(k):
        return (t, z * 2 + k // nd, k % nd)

    barrier = pltpu.get_barrier_semaphore()

    def greet(where):
        pl.semaphore_signal(barrier, inc=1, device_id=where, device_id_type=MESH)

    for k in range(1, nt):
        greet(((t + k) % nt, h, d))
    for hh in (h_next, h_prev):
        for tt in (t_prev, t, t_next):
            greet((tt, hh, d))
    for k in range(nt // 2):
        greet((2 * k + 1, h_prev, d))

    @pl.when(core == 1)
    def _():
        for k in range(nt):
            greet((k, h_next, d))

    for k in range(1, ny):
        greet(at_y((y + k) % ny))
    for k in range(1, nz):
        greet((t, ((z + k) % nz) * 2 + h % 2, d))

    by_column[...] = column_order(256)
    og_in.wait()
    x_in.wait()
    x_own = jnp.dot(by_column[...], x_ref[...], preferred_element_type=F32).astype(BF16)
    xe[2:4, 1:5] = x_own.reshape(2, 4, 32, 256)
    oge[0, 1:3] = og_ref[...].reshape(2, 16, 256)

    def keep_halves(block, out, rows):
        moved = jnp.dot(block, by_channel[...], preferred_element_type=F32).astype(BF16)
        for k in range(2):
            out[k] = moved[:, 128 * k : 128 * (k + 1)].reshape(2, rows, 32, 128)

    greetings = (nt - 1) + 6 + (ny - 1) + (nz - 1) + nt // 2
    pl.semaphore_wait(barrier, greetings + core * nt)

    def send(src, dst, ssem, rsem, where):
        return pltpu.make_async_remote_copy(
            src_ref=src, dst_ref=dst, send_sem=ssem, recv_sem=rsem, device_id=where, device_id_type=MESH
        )

    def p1(k, src, dst, where):
        return send(src, dst, p1s.at[k], p1r.at[k], where)

    og_halo = [
        p1(0, oge.at[0:1, 1:3], oge.at[1:2, 1:3], (t_prev, h, d)),
        p1(1, oge.at[0:1, 2:3], oge.at[0:1, 0:1], (t, h_next, d)),
        p1(2, oge.at[0:1, 2:3], oge.at[1:2, 0:1], (t_prev, h_next, d)),
    ]
    x_halo = [
        p1(3, xe.at[2:4, 1:5], xe.at[0:2, 1:5], (t_next, h, d)),
        p1(4, xe.at[2:4, 4:5], xe.at[2:4, 0:1], (t, h_next, d)),
        p1(5, xe.at[2:4, 1:2], xe.at[2:4, 5:6], (t, h_prev, d)),
        p1(6, xe.at[2:4, 4:5], xe.at[0:2, 0:1], (t_next, h_next, d)),
        p1(7, xe.at[2:4, 1:2], xe.at[0:2, 5:6], (t_next, h_prev, d)),
    ]
    for c in og_halo + x_halo:
        c.start()

    def gather_sends(role, source, target, ssem, rsem, to_h=None):
        rim = to_h is not None
        to_h = to_h if rim else h
        for k in range(nt // 2):
            to_chip = (chip + k) % (nt // 2)
            to = to_chip * 2 + role
            c = send(source(to_chip), target(t), ssem.at[k], rsem.at[t], (to, to_h, d))
            if k == 0 and not rim:
                pl.when(core != role)(c.start)
            else:
                c.start()

    def gather_sent(role, source, target, ssem, rsem, to_h=None):
        rim = to_h is not None
        to_h = to_h if rim else h
        for k in range(nt // 2):
            to_chip = (chip + k) % (nt // 2)
            to = to_chip * 2 + role
            c = send(source(to_chip), target(t), ssem.at[k], rsem.at[t], (to, to_h, d))
            if k == 0 and not rim:
                pl.when(core != role)(c.wait_send)
            else:
                c.wait_send()

    def gather_received(source, target, ssem, rsem, from_h=None):
        for k in range(0 if from_h is not None else 1, nt):
            s = (t + k) % nt
            where = (s, h if from_h is None else from_h, d)
            send(source(0), target(s), ssem.at[0], rsem.at[s], where).wait_recv()

    def later_frames(ref):
        return lambda s: ref.at[pl.ds(2 + 2 * s, 2)]

    og_move = (lambda c: oge.at[0, 1:3], lambda s: ogat.at[s], oss, osr)
    x_move = (lambda c: xs.at[c // 2], later_frames(xg), xss, xsr)
    x_rim_move = (lambda c: xsh.at[c // 2], later_frames(xgh), xhs, xhr)
    g_move = (lambda c: gs.at[c % 2], lambda s: gg.at[pl.ds(2 * s, 2)], gss, gsr)
    h_move = (lambda c: hs.at[c], later_frames(hgat), hss, hsr)
    h_rim_move = (lambda c: hsh.at[c], later_frames(hgh), hhs, hhr)
    gather_sends(1, *og_move)

    by_channel[...] = channel_order(256)
    keep_halves(x_own, xs, 4)
    by_quarter[...] = quarter_order(256)
    part[pl.ds(27 * 128, 8)] = jnp.zeros((8, 128), F32)
    part4[pl.ds(27 * 64, 8)] = jnp.zeros((8, 256), F32)
    for c in og_halo:
        c.wait_recv()
    gather_sends(0, *x_move)
    for c in x_halo:
        c.wait_recv()

    @pl.when(h == 0)
    def _():
        xe[:, 0] = jnp.zeros((4, 32, 256), BF16)

    @pl.when(h == nh - 1)
    def _():
        xe[:, 5] = jnp.zeros((4, 32, 256), BF16)

    @pl.when(first)
    def _():
        xe[0] = xe[2]
        xe[1] = xe[2]

    rims = jnp.concatenate([xe[2:4, 0:1], xe[2:4, 5:6]], axis=1)
    keep_halves(rims.reshape(128, 256), xsh, 2)
    gather_sends(0, *x_rim_move)

    wc1.wait()
    sums = [None] * 3
    for a in range(3):
        for b in range(3):
            lhs = xe[a : a + 2, b : b + 4].reshape(256, 256)
            for e in range(3):
                q = jnp.dot(lhs, w1[a * 9 + b * 3 + e], preferred_element_type=F32)
                sums[e] = q if sums[e] is None else sums[e] + q
    value = from_left(sums[0]) + sums[1] + from_right(sums[2])
    sigmoid = jax.nn.sigmoid(value)
    he[2:4, 0:4] = (value * sigmoid).astype(BF16).reshape(2, 4, 32, 256)
    zs[0] = sigmoid * (1.0 + value * (1.0 - sigmoid))

    def p2(k, src, dst, where):
        return send(src, dst, p2s.at[k], p2r.at[k], where)

    h_rows = p2(0, he.at[2:4, 0:1], he.at[2:4, 4:5], (t, h_prev, d))
    g_rows = [
        p2(1, ge.at[0:2, 4:5], ge.at[0:2, 0:1], (t, h_next, d)),
        p2(2, ge.at[0:2, 1:2], ge.at[0:2, 5:6], (t, h_prev, d)),
    ]
    h_frames = p2(3, he.at[2:4], he.at[0:2], (t_next, h, d))
    g_frames = p2(4, ge.at[0:2], ge.at[2:4], (t_prev, h, d))
    def keep_quarters(block, out, rows):
        lanes = [block[..., p : p + 16, :].reshape(32 * rows, 256) for p in (0, 16)]
        both = jnp.concatenate(lanes, axis=1)
        moved = jnp.dot(both, by_quarter[...], preferred_element_type=F32).astype(BF16)
        for k in range(4):
            out[k] = moved[:, 128 * k : 128 * (k + 1)].reshape(2, rows, 16, 128)

    keep_quarters(he[2:4, 0:4], hs, 4)
    for k in range(4):
        hsh[k] = hs[k, :, 0:1]
    gather_sends(1, *h_rim_move, h_prev)
    gather_sends(1, *h_move)
    h_rows.start()

    wc2.wait()

    @pl.when(t == nt - 1)
    def _():
        oge[1] = jnp.zeros((3, 16, 256), BF16)

    @pl.when(h == 0)
    def _():
        oge[:, 0] = jnp.zeros((2, 16, 256), BF16)

    og_rows = oge[...].reshape(96, 256)

    def spread_og(a, b, e):
        lhs = og_rows if a < 2 else og_rows[:48]
        q = lax.dot_general(lhs, w2[a * 9 + b * 3 + e], NT, preferred_element_type=F32)
        offset = 0 if b == 2 else 16
        here, later = q[offset : offset + 32], q[48 + offset : 48 + offset + 32]
        return (jnp.where(first, here, 0.0), later) if a < 2 else (here, None)

    early = {}
    for f in (1, 0):
        terms = dict(early)
        for a in (1,) if f else (0, 2):
            for b in range(3):
                for e in range(3):
                    key = (b % 2, e)
                    here, later = spread_og(a, b, e)
                    if f:
                        early[key] = early.get(key, 0.0) + here
                        terms[key] = terms.get(key, 0.0) + later
                    else:
                        terms[key] = terms[key] + (here if a else here + later)
        for b in range(2):
            even = terms[b, 0] + move_in_16(terms[b, 2], 1)
            odd = terms[b, 1]
            for u in range(2):
                hg[f, 2 * u + b, 0:16] = even[16 * u : 16 * u + 16]
                hg[f, 2 * u + b, 16:32] = odd[16 * u : 16 * u + 16]
        grad = (hg[f].reshape(128, 256) * zs[0, 128 * f : 128 * f + 128]).astype(BF16)
        ge[f, 1:5] = grad.reshape(4, 32, 256)
        for k in range(2):
            gs[k, f] = grad[:, 128 * k : 128 * (k + 1)].reshape(4, 32, 128)
    gather_sends(0, *g_move)
    for c in g_rows:
        c.start()

    @pl.when(core == 0)
    def _():
        xg[pl.ds(2 + 2 * t, 2)] = xs[chip // 2]
        xgh[pl.ds(2 + 2 * t, 2)] = xsh[chip // 2]
        gg[pl.ds(2 * t, 2)] = gs[chip % 2]
        gather_received(*x_move)
        gather_received(*x_rim_move)
        for f in range(2):
            xg[f] = xg[2]
            xgh[f] = xgh[2]

        def turn(f, carry):
            rows = jnp.concatenate([xgh[f, 0:1], xg[f], xgh[f, 1:2]], axis=0)
            for b in range(3):
                xt[f, 128 * b : 128 * (b + 1)] = rows[b : b + 4].reshape(128, 128).T
            return carry

        lax.fori_loop(0, 2 * nt + 2, turn, 0)
        gather_received(*g_move)

        def spread(s, carry):
            rows = pl.ds(pl.multiple_of(256 * s, 256), 256)
            g = gg[pl.ds(2 * s, 2)].reshape(256, 128)
            wide = g.astype(F32)
            g3[rows, 0:128] = from_right(wide).astype(BF16)
            g3[rows, 128:256] = g
            g3[rows, 256:384] = from_left(wide).astype(BF16)
            return carry

        lax.fori_loop(0, nt, spread, 0)

    @pl.when(core == 1)
    def _():
        hgat[pl.ds(2 + 2 * t, 2)] = hs[chip]
        ogat[t] = oge[0, 1:3]
        gather_received(*og_move)
        og_all = ogat[...].reshape(32 * nt, 256)
        og_two = jnp.concatenate([og_all, move_in_16(og_all.astype(F32), 1).astype(BF16)], axis=1)
        gather_received(*h_move)
        gather_received(*h_rim_move, h_next)

        @pl.when(h == nh - 1)
        def _():
            hgh[...] = jnp.zeros(hgh.shape, BF16)

        for f in range(2):
            hgat[f] = hgat[2]
            hgh[f] = hgh[2]
        for a in range(3):
            for b in range(3):
                pieces = [
                    hgh[2 * f + a, 0] if b + 2 * r == 4 else hgat[2 * f + a, b + 2 * r]
                    for f in range(nt)
                    for r in range(2)
                ]
                lhs = jnp.concatenate(pieces, axis=0)
                q = lax.dot_general(lhs, og_two, TN, preferred_element_type=F32)
                n = 64 * (a * 9 + b * 3)
                part4[n : n + 64] = q[0:64, 0:256]
                part4[n + 64 : n + 128] = q[64:128, 0:256]
                part4[n + 128 : n + 192] = q[0:64, 256:512]

    def coded(codes):
        code = codes[0]
        for k in range(1, nz):
            code = jnp.where(z == k, codes[k], code)
        return code

    chunk_code = coded(
        (0o1276534, 0o10276534, 0o21034576, 0o32451067,
         0o43526710, 0o56743201, 0o67543201, 0o76501243)
    )
    tap_code = coded((0o21, 0o21, 0o12, 0o102, 0o120, 0o210, 0o210, 0o201))

    def chunk_at(j):
        return chunk_code // 8**j % 8

    def tap_at(j):
        return tap_code // 8**j % 8

    def y_copies(i):
        two = pl.ds(2 * i, 2)
        return [
            send(
                sl.at[(y + k) % ny, two], r1.at[k - 1, two],
                rs1s.at[i, k - 1], rs1r.at[i, k - 1], at_y((y + k) % ny),
            )
            for k in (2, 1, 3)
        ]

    def send_chunks(i):
        def cut(m, carry):
            j, k = 2 * i + m // ny, m % ny
            c = chunk_at(j)
            n = groups * (c * ny + k)

            @pl.when(core == 0)
            def _():
                first_row = pl.multiple_of((n + 1 - chip // 2) // 2 * 8, 8)
                sl[k, j] = part[pl.ds(first_row, slot)].astype(BF16)

            @pl.when(core == 1)
            def _():
                first_row = pl.multiple_of((n + 3 - chip) // 4 * 8, 8)
                rows = part4[pl.ds(first_row, slot // 2)]
                stacked = jnp.concatenate([rows[:, :128], rows[:, 128:]], axis=0)
                sl[k, j] = stacked.astype(BF16)

            return carry

        lax.fori_loop(0, 2 * ny, cut, 0)
        for copy in y_copies(i):
            copy.start()


    for k in range(3):

        @pl.when(core == 0)
        def _():
            a = tap_at(k)
            lhs = jnp.concatenate([xt[a + f] for f in range(2 * nt)], axis=1)
            q = jnp.dot(lhs, g3[...], preferred_element_type=F32)
            for b in range(3):
                for e in range(3):
                    n = pl.multiple_of(128 * (a * 9 + b * 3 + e), 128)
                    part[pl.ds(n, 128)] = q[128 * b : 128 * (b + 1), 128 * e : 128 * (e + 1)]

        send_chunks(k)
    send_chunks(3)
    h_rows.wait_recv()
    for c in g_rows:
        c.wait_recv()

    @pl.when(h == 0)
    def _():
        ge[0:2, 0] = jnp.zeros((2, 32, 256), BF16)

    @pl.when(h == nh - 1)
    def _():
        he[2:4, 4] = jnp.zeros((2, 32, 256), BF16)
        ge[0:2, 5] = jnp.zeros((2, 32, 256), BF16)

    h_frames.start()
    g_frames.start()


    def z_copy(j):
        c = chunk_at(j)
        k = (c - z + nz) % nz - 1
        where = (t, c * 2 + h % 2, d)
        return send(s1.at[c], r2.at[k], rs2s.at[k], rs2r.at[k], where)

    def pass_chunks(i):
        for copy in y_copies(i):
            copy.wait_recv()
        for j in (2 * i, 2 * i + 1):
            total = sl[y, j].astype(F32)
            for n in range(ny - 1):
                total = total + r1[n, j].astype(F32)
            s1[chunk_at(j)] = total.astype(BF16)
            if j < nz - 1:
                z_copy(j).start()

    h_frames.wait_recv()

    @pl.when(first)
    def _():
        he[0] = he[2]
        he[1] = he[2]

    sums = [None] * 3
    for a in range(3):
        for b in range(3):
            for e in range(3):
                p = 16 * (e % 2)
                lhs = jnp.concatenate([he[a, b, p : p + 16], he[a, b + 2, p : p + 16]], axis=0)
                q = jnp.dot(lhs, w2[a * 9 + b * 3 + e], preferred_element_type=F32)
                sums[e] = q if sums[e] is None else sums[e] + q
    enc_ref[...] = (sums[0] + sums[1] + move_in_16(sums[2], -1)).astype(BF16)
    pass_chunks(0)
    pass_chunks(1)

    pass_chunks(2)
    pass_chunks(3)

    g_frames.wait_recv()

    @pl.when(t == nt - 1)
    def _():
        ge[2:4] = jnp.zeros((2, 6, 32, 256), BF16)

    sums = [None] * 3
    for a in range(3):
        for b in range(3):
            lhs = ge[2 - a : 4 - a, 2 - b : 6 - b].reshape(256, 256)
            for e in range(3):
                q = lax.dot_general(lhs, w1[a * 9 + b * 3 + e], NT, preferred_element_type=F32)
                sums[e] = q if sums[e] is None else sums[e] + q
    for e in range(3):
        zs[e] = sums[e]

    @pl.when(first)
    def _():
        for e in range(3):
            total = zs[e, 0:128]
            for a, f in ((0, 0), (0, 1), (1, 0)):
                for b in range(3):
                    lhs = ge[f, 2 - b : 6 - b].reshape(128, 256)
                    total = total + lax.dot_general(
                        lhs, w1[a * 9 + b * 3 + e], NT, preferred_element_type=F32
                    )
            zs[e, 0:128] = total

    clip = (from_right(zs[0]) + zs[1] + from_left(zs[2])).astype(BF16)
    clip_ref[...] = lax.dot_general(
        by_column[...], clip, TN, preferred_element_type=F32
    ).astype(BF16)

    total = s1[z].astype(F32)
    for k in range(1, nz):
        source = ((z - k + nz) % nz * 2 + h % 2, d)
        send(
            s1.at[z], r2.at[k - 1], rs2s.at[k - 1], rs2r.at[k - 1], (t, *source)
        ).wait_recv()
        total = total + r2[k - 1].astype(F32)
    fs[...] = total.astype(BF16)
    t_sends = []
    for k in range(1, nt):
        where = ((t + k) % nt, h, d)
        t_sends.append(send(fs, fg.at[t], ags.at[k - 1], agr.at[k - 1], where))
    for c in t_sends:
        c.start()
    fg[t] = fs[...]
    for k in range(1, nt):
        s = (t + nt - k) % nt
        send(fs, fg.at[s], ags.at[k - 1], agr.at[k - 1], (s, h, d)).wait_recv()

    for c in og_halo + x_halo + [h_rows] + g_rows + [h_frames, g_frames] + t_sends:
        c.wait_send()
    for i in range(nz // 2):
        for copy in y_copies(i):
            copy.wait_send()
    for j in range(nz - 1):
        z_copy(j).wait_send()
    for move in (x_move, x_rim_move, g_move):
        gather_sent(0, *move)
    for move in (og_move, h_move):
        gather_sent(1, *move)
    gather_sent(1, *h_rim_move, h_prev)


def finish(sizes, enc_ref, clip_ref, fg, enc_hbm, clip_hbm, conv_hbm, down_hbm, ff, conv, down, sem):
    nt, nh, nd = sizes
    block = lax.axis_index("height") * nd + lax.axis_index("dp")
    groups = 864 // (nh * nd)
    slot = fg.shape[1]
    early = [
        pltpu.make_async_copy(enc_ref, enc_hbm, sem.at[0]),
        pltpu.make_async_copy(clip_ref, clip_hbm, sem.at[1]),
    ]
    for c in early:
        c.start()
    cells = nt * nh * nd * 256
    scale = (1.0 / math.sqrt(cells), 1.0 / math.sqrt(cells // 8))
    for s in range(nt):
        ff[s] = fg[s].astype(F32) * scale[s % 2]
    late = []
    for k, (out, hbm) in enumerate(((conv, conv_hbm), (down, down_hbm))):
        for j in range(groups):
            n = groups * block + j
            for o in range(2):
                if k == 0:
                    rows = ff[2 * (2 * (n % 2) + o), 8 * (j // 2) : 8 * (j // 2) + 8]
                else:
                    row = o * (slot // 2) + 8 * (j // 4)
                    rows = ff[2 * (n % 4) + 1, row : row + 8]
                out[8 * j : 8 * j + 8, 128 * o : 128 * o + 128] = rows
        c = pltpu.make_async_copy(out, hbm, sem.at[2 + k])
        c.start()
        late.append(c)
    for c in early + late:
        c.wait()


def body(mesh_sizes, video_clip, conv_weight, down_weight, output_grad):
    nt, nh, nd = mesh_sizes
    ny, nz = 2 * nd, nh // 2
    blocks = ny * nz
    groups = 864 // blocks
    slot = 8 * ((groups + 1) // 2)
    dma = pltpu.SemaphoreType.DMA

    def vm(*shape, dtype=BF16):
        return pltpu.VMEM(shape, dtype)

    scratch = [
        vm(256, 256), vm(256, 256), vm(512, 512), vm(256, 256), vm(32, 256), vm(27, 256, 256), vm(27, 256, 256),
        vm(4, 6, 32, 256), vm(2, 3, 16, 256), vm(4, 5, 32, 256), vm(4, 6, 32, 256),
        vm(2, 4, 32, 256, dtype=F32), vm(3, 256, 256, dtype=F32),
        vm(2, 2, 4, 32, 128), vm(2, 2, 2, 32, 128), vm(2, 2, 4, 32, 128),
        vm(4, 2, 4, 16, 128), vm(4, 2, 1, 16, 128),
        vm(2 * nt + 2, 4, 32, 128), vm(2 * nt + 2, 2, 32, 128), vm(2 * nt, 4, 32, 128),
        vm(2 * nt + 2, 4, 16, 128), vm(2 * nt + 2, 1, 16, 128), vm(nt, 2, 16, 256),
        vm(2 * nt + 2, 384, 128), vm(256 * nt, 384),
        vm(27 * 128 + 8, 128, dtype=F32), vm(27 * 64 + 8, 256, dtype=F32),
        vm(ny, nz, slot, 128), vm(ny - 1, nz, slot, 128),
        vm(nz, slot, 128), vm(nz - 1, slot, 128),
        vm(slot, 128),
        dma((4,)), dma((8,)), dma((8,)), dma((5,)), dma((5,)),
    ]
    scratch += [dma((n,)) for _ in range(6) for n in (nt // 2, nt)]
    scratch += [dma(n) for n in ((nz // 2, ny - 1),) * 2 + ((nz - 1,),) * 2 + ((nt - 1,),) * 2]
    vmem = pl.BlockSpec(memory_space=pltpu.VMEM)
    hbm = pl.BlockSpec(memory_space=pltpu.HBM)
    shape = jax.ShapeDtypeStruct
    features = (shape((32, 256), BF16), shape((256, 256), BF16))
    gathered = pl.pallas_call(
        functools.partial(kernel, mesh_sizes),
        out_shape=(*features, shape((nt, slot, 128), BF16)),
        in_specs=[hbm] * 4,
        out_specs=(vmem,) * 3,
        scratch_shapes=scratch,
        compiler_params=pltpu.CompilerParams(
            collective_id=0, has_side_effects=True, vmem_limit_bytes=44 * 2**20
        ),
    )(
        *(
            pltpu.with_memory_space_constraint(operand, pltpu.HBM)
            for operand in (
                video_clip.reshape(256, 256),
                conv_weight.reshape(27, 256, 256),
                down_weight.reshape(27, 256, 256),
                output_grad.reshape(32, 256),
            )
        )
    )
    rows = shape((groups * 8, 256), F32)
    enc, clip, conv, down = pl.pallas_call(
        functools.partial(finish, mesh_sizes),
        out_shape=(*features, rows, rows),
        in_specs=[vmem] * 3,
        out_specs=(hbm,) * 4,
        scratch_shapes=[
            vm(nt, slot, 128, dtype=F32),
            vm(groups * 8, 256, dtype=F32),
            vm(groups * 8, 256, dtype=F32),
            dma((4,)),
        ],
        compiler_params=pltpu.CompilerParams(vmem_limit_bytes=16 * 2**20),
    )(*gathered)
    return enc.reshape(1, 1, 2, 16, 256), clip.reshape(1, 2, 4, 32, 256), conv, down


def solution(mesh):
    sizes = tuple(mesh.shape[a] for a in ("tm", "height", "dp"))
    cells = P("dp", "tm", "height", None, None)
    rows = P(("height", "dp"), None)
    return jax.shard_map(
        functools.partial(body, sizes),
        mesh=mesh,
        in_specs=(cells, P(), P(), cells),
        out_specs=(cells, cells, rows, rows),
        check_vma=False,
    )
```

```python
import functools
import math

import jax
import jax.numpy as jnp
from jax import lax
from jax.experimental import pallas as pl
from jax.experimental.pallas import tpu as pltpu
from jax.sharding import PartitionSpec as P

MESH = pl.DeviceIdType.MESH
F32 = jnp.float32
BF16 = jnp.bfloat16
NT = (((1,), (1,)), ((), ()))
TN = (((0,), (0,)), ((), ()))


def iota2(shape, dim):
    return lax.broadcasted_iota(jnp.int32, shape, dim)


def one_hot(mask):
    return jnp.where(mask, 1.0, 0.0).astype(F32).astype(BF16)


def column_order(n):
    m, k = iota2((n, n), 0), iota2((n, n), 1)
    return one_hot(k == (m & ~31) + 2 * (m & 15) + ((m >> 4) & 1))


def channel_order(n):
    i, k = iota2((n, n), 0), iota2((n, n), 1)
    j = k & 127
    return one_hot(i == (j >> 3) * 16 + (k >> 7) * 8 + (j & 7))


def quarter_order(n):
    i, k = iota2((2 * n, 2 * n), 0), iota2((2 * n, 2 * n), 1)
    j = k & 63
    return one_hot(i == ((k >> 6) & 1) * n + (j >> 3) * 32 + (k >> 7) * 8 + (j & 7))


def move_in_16(x, step):
    n = x.shape[0]
    k = iota2(x.shape, 0) & 15
    rolled = pltpu.roll(x, step % n, 0)
    return jnp.where(k == (0 if step == 1 else 15), 0.0, rolled)


def halves(x):
    groups = x.shape[0] // 32
    parts = x.reshape(groups, 2, 16, x.shape[1])
    return parts[:, 0].reshape(groups * 16, -1), parts[:, 1].reshape(groups * 16, -1)


def joined(even, odd):
    groups = even.shape[0] // 16
    parts = [h.reshape(groups, 1, 16, h.shape[1]) for h in (even, odd)]
    return jnp.concatenate(parts, axis=1).reshape(groups * 32, -1)


def from_left(x):
    even, odd = halves(x)
    return joined(move_in_16(odd, 1), even)


def from_right(x):
    even, odd = halves(x)
    return joined(odd, move_in_16(even, -1))


def kernel(
    sizes,
    x_hbm, w1_hbm, w2_hbm, og_hbm,
    enc_ref, clip_ref, fg,
    by_column, by_channel, by_quarter, x_ref, og_ref, w1, w2, xe, oge, he, ge, hg, zs,
    xs, xsh, gs, hs, hsh, xg, xgh, gg, hgat, hgh, ogat, xt, g3, part, part4,
    sl, r1, s1, r2, q1, q2, q3, fs,
    wsem, p1s, p1r, p2s, p2r,
    xss, xsr, xhs, xhr, gss, gsr, hss, hsr, hhs, hhr, oss, osr,
    rs1s, rs1r, rs2s, rs2r, q1s, q1r, q2s, q2r, ags, agr,
):
    nt, nh, nd = sizes
    ny, nz = 2 * nd, nh // 2
    t, h, d = lax.axis_index("tm"), lax.axis_index("height"), lax.axis_index("dp")
    y, z = (h % 2) * nd + d, h // 2
    core, chip = t % 2, t // 2
    t_next, t_prev = (t + 1) % nt, (t + nt - 1) % nt
    h_next, h_prev = (h + 1) % nh, (h + nh - 1) % nh
    block = z * ny + y
    groups = 864 // (ny * nz)
    slot = 8 * ((groups + 1) // 2)

    wc1 = pltpu.make_async_copy(w1_hbm, w1, wsem.at[0])
    wc2 = pltpu.make_async_copy(w2_hbm, w2, wsem.at[1])
    first = t == 0
    og_in = pltpu.make_async_copy(og_hbm, og_ref, wsem.at[2])
    x_in = pltpu.make_async_copy(x_hbm, x_ref, wsem.at[3])
    for c in (x_in, og_in, wc2, wc1):
        c.start()

    def at_y(k):
        return (t, z * 2 + k // nd, k % nd)

    barrier = pltpu.get_barrier_semaphore()

    def greet(where):
        pl.semaphore_signal(barrier, inc=1, device_id=where, device_id_type=MESH)

    for k in range(1, nt):
        greet(((t + k) % nt, h, d))
    for k in range(nt // 2):
        greet((2 * k + 1, h_prev, d))

    @pl.when(core == 0)
    def _():
        greet((t, h_prev, d))
        for k in (t_prev, t, t_next):
            greet((k, h_next, d))

    @pl.when(core == 1)
    def _():
        greet((t_prev, h_prev, d))
        greet((t_next, h_prev, d))
        for k in range(nt):
            greet((k, h_next, d))

    for k in range(1, ny):
        greet(at_y((y + k) % ny))
    for k in range(1, nz):
        greet((t, ((z + k) % nz) * 2 + h % 2, d))

    by_column[...] = column_order(256)
    og_in.wait()
    x_in.wait()
    x_own = jnp.dot(by_column[...], x_ref[...], preferred_element_type=F32).astype(BF16)
    xe[2:4, 1:5] = x_own.reshape(2, 4, 32, 256)
    oge[0, 1:3] = og_ref[...].reshape(2, 16, 256)

    def keep_halves(block, out, rows):
        moved = jnp.dot(block, by_channel[...], preferred_element_type=F32).astype(BF16)
        for k in range(2):
            out[k] = moved[:, 128 * k : 128 * (k + 1)].reshape(2, rows, 32, 128)

    greetings = (nt - 1) + (ny - 1) + (nz - 1) + nt // 2 + 4
    pl.semaphore_wait(barrier, greetings + core * (nt - 2))

    def send(src, dst, ssem, rsem, where):
        return pltpu.make_async_remote_copy(
            src_ref=src, dst_ref=dst, send_sem=ssem, recv_sem=rsem, device_id=where, device_id_type=MESH
        )

    def p1(k, src, dst, where):
        return send(src, dst, p1s.at[k], p1r.at[k], where)

    og_halo = [
        p1(0, oge.at[0:1, 1:3], oge.at[1:2, 1:3], (t_prev, h, d)),
        p1(1, oge.at[0:1, 2:3], oge.at[0:1, 0:1], (t, h_next, d)),
        p1(2, oge.at[0:1, 2:3], oge.at[1:2, 0:1], (t_prev, h_next, d)),
    ]
    x_halo = [
        p1(3, xe.at[2:4, 1:5], xe.at[0:2, 1:5], (t_next, h, d)),
        p1(4, xe.at[2:4, 4:5], xe.at[2:4, 0:1], (t, h_next, d)),
        p1(5, xe.at[2:4, 1:2], xe.at[2:4, 5:6], (t, h_prev, d)),
        p1(6, xe.at[2:4, 4:5], xe.at[0:2, 0:1], (t_next, h_next, d)),
        p1(7, xe.at[2:4, 1:2], xe.at[0:2, 5:6], (t_next, h_prev, d)),
    ]
    for c in og_halo + x_halo:
        c.start()

    def gather_sends(role, source, target, ssem, rsem, to_h=None):
        rim = to_h is not None
        to_h = to_h if rim else h
        for k in range(nt // 2):
            to_chip = (chip + k) % (nt // 2)
            to = to_chip * 2 + role
            c = send(source(to_chip), target(t), ssem.at[k], rsem.at[t], (to, to_h, d))
            if k == 0 and not rim:
                pl.when(core != role)(c.start)
            else:
                c.start()

    def gather_sent(role, source, target, ssem, rsem, to_h=None):
        rim = to_h is not None
        to_h = to_h if rim else h
        for k in range(nt // 2):
            to_chip = (chip + k) % (nt // 2)
            to = to_chip * 2 + role
            c = send(source(to_chip), target(t), ssem.at[k], rsem.at[t], (to, to_h, d))
            if k == 0 and not rim:
                pl.when(core != role)(c.wait_send)
            else:
                c.wait_send()

    def gather_received(source, target, ssem, rsem, from_h=None):
        for k in range(0 if from_h is not None else 1, nt):
            s = (t + k) % nt
            where = (s, h if from_h is None else from_h, d)
            send(source(0), target(s), ssem.at[0], rsem.at[s], where).wait_recv()

    def later_frames(ref):
        return lambda s: ref.at[pl.ds(2 + 2 * s, 2)]

    og_move = (lambda c: oge.at[0, 1:3], lambda s: ogat.at[s], oss, osr)
    x_move = (lambda c: xs.at[c // 2], later_frames(xg), xss, xsr)
    x_rim_move = (lambda c: xsh.at[c // 2], later_frames(xgh), xhs, xhr)
    g_move = (lambda c: gs.at[c % 2], lambda s: gg.at[pl.ds(2 * s, 2)], gss, gsr)
    h_move = (lambda c: hs.at[c], later_frames(hgat), hss, hsr)
    h_rim_move = (lambda c: hsh.at[c], later_frames(hgh), hhs, hhr)
    gather_sends(1, *og_move)

    by_channel[...] = channel_order(256)
    keep_halves(x_own, xs, 4)
    by_quarter[...] = quarter_order(256)
    part[pl.ds(27 * 128, 8)] = jnp.zeros((8, 128), F32)
    part4[pl.ds(27 * 64, 8)] = jnp.zeros((8, 256), F32)
    for c in og_halo:
        c.wait_recv()
    gather_sends(0, *x_move)

    wc2.wait()

    @pl.when(t == nt - 1)
    def _():
        oge[1] = jnp.zeros((3, 16, 256), BF16)

    @pl.when(h == 0)
    def _():
        oge[:, 0] = jnp.zeros((2, 16, 256), BF16)

    og_rows = oge[...].reshape(96, 256)
    terms = {}
    for e in range(3):
        for a in range(3):
            for b in range(3):
                lhs = og_rows if a < 2 else og_rows[:48]
                q = lax.dot_general(lhs, w2[a * 9 + b * 3 + e], NT, preferred_element_type=F32)
                offset = 0 if b == 2 else 16
                here = q[offset : offset + 32]
                if a < 2:
                    here = jnp.where(first, here, 0.0)
                    later = q[48 + offset : 48 + offset + 32]
                    key = (a, b % 2, e)
                    terms[key] = terms.get(key, 0.0) + later
                key = (0, b % 2, e)
                terms[key] = terms.get(key, 0.0) + here
    for f in range(2):
        for b in range(2):
            even = terms[f, b, 0] + move_in_16(terms[f, b, 2], 1)
            odd = terms[f, b, 1]
            for u in range(2):
                hg[f, 2 * u + b, 0:16] = even[16 * u : 16 * u + 16]
                hg[f, 2 * u + b, 16:32] = odd[16 * u : 16 * u + 16]

    for c in x_halo:
        c.wait_recv()

    @pl.when(h == 0)
    def _():
        xe[:, 0] = jnp.zeros((4, 32, 256), BF16)

    @pl.when(h == nh - 1)
    def _():
        xe[:, 5] = jnp.zeros((4, 32, 256), BF16)

    @pl.when(first)
    def _():
        xe[0] = xe[2]
        xe[1] = xe[2]

    rims = jnp.concatenate([xe[2:4, 0:1], xe[2:4, 5:6]], axis=1)
    keep_halves(rims.reshape(128, 256), xsh, 2)
    gather_sends(0, *x_rim_move)

    wc1.wait()
    sums = [None] * 3
    for a in range(3):
        for b in range(3):
            lhs = xe[a : a + 2, b : b + 4].reshape(256, 256)
            for e in range(3):
                q = jnp.dot(lhs, w1[a * 9 + b * 3 + e], preferred_element_type=F32)
                sums[e] = q if sums[e] is None else sums[e] + q
    value = from_left(sums[0]) + sums[1] + from_right(sums[2])
    sigmoid = jax.nn.sigmoid(value)
    he[2:4, 0:4] = (value * sigmoid).astype(BF16).reshape(2, 4, 32, 256)
    zs[0] = sigmoid * (1.0 + value * (1.0 - sigmoid))

    def p2(k, src, dst, where):
        return send(src, dst, p2s.at[k], p2r.at[k], where)

    h_rows = p2(0, he.at[2:4, 0:1], he.at[2:4, 4:5], (t, h_prev, d))
    g_rows = [
        p2(1, ge.at[0:2, 4:5], ge.at[0:2, 0:1], (t, h_next, d)),
        p2(2, ge.at[0:2, 1:2], ge.at[0:2, 5:6], (t, h_prev, d)),
    ]
    h_frames = p2(3, he.at[2:4], he.at[0:2], (t_next, h, d))
    g_frames = p2(4, ge.at[0:2], ge.at[2:4], (t_prev, h, d))
    def keep_quarters(block, out, rows):
        lanes = [block[..., p : p + 16, :].reshape(32 * rows, 256) for p in (0, 16)]
        both = jnp.concatenate(lanes, axis=1)
        moved = jnp.dot(both, by_quarter[...], preferred_element_type=F32).astype(BF16)
        for k in range(4):
            out[k] = moved[:, 128 * k : 128 * (k + 1)].reshape(2, rows, 16, 128)

    for f in (1, 0):
        grad = (hg[f].reshape(128, 256) * zs[0, 128 * f : 128 * f + 128]).astype(BF16)
        ge[f, 1:5] = grad.reshape(4, 32, 256)
        for k in range(2):
            gs[k, f] = grad[:, 128 * k : 128 * (k + 1)].reshape(4, 32, 128)
    gather_sends(0, *g_move)
    keep_quarters(he[2:4, 0:4], hs, 4)
    for k in range(4):
        hsh[k] = hs[k, :, 0:1]
    gather_sends(1, *h_rim_move, h_prev)
    gather_sends(1, *h_move)
    h_rows.start()
    for c in g_rows:
        c.start()

    @pl.when(core == 0)
    def _():
        xg[pl.ds(2 + 2 * t, 2)] = xs[chip // 2]
        xgh[pl.ds(2 + 2 * t, 2)] = xsh[chip // 2]
        gg[pl.ds(2 * t, 2)] = gs[chip % 2]
        gather_received(*x_move)
        gather_received(*x_rim_move)
        for f in range(2):
            xg[f] = xg[2]
            xgh[f] = xgh[2]

        def turn(f, carry):
            rows = jnp.concatenate([xgh[f, 0:1], xg[f], xgh[f, 1:2]], axis=0)
            for b in range(3):
                xt[f, 128 * b : 128 * (b + 1)] = rows[b : b + 4].reshape(128, 128).T
            return carry

        lax.fori_loop(0, 2 * nt + 2, turn, 0)
        gather_received(*g_move)

        def spread(s, carry):
            rows = pl.ds(pl.multiple_of(256 * s, 256), 256)
            g = gg[pl.ds(2 * s, 2)].reshape(256, 128)
            wide = g.astype(F32)
            g3[rows, 0:128] = from_right(wide).astype(BF16)
            g3[rows, 128:256] = g
            g3[rows, 256:384] = from_left(wide).astype(BF16)
            return carry

        lax.fori_loop(0, nt, spread, 0)

    @pl.when(core == 1)
    def _():
        hgat[pl.ds(2 + 2 * t, 2)] = hs[chip]
        ogat[t] = oge[0, 1:3]
        gather_received(*og_move)
        og_all = ogat[...].reshape(32 * nt, 256)
        og_two = jnp.concatenate([og_all, move_in_16(og_all.astype(F32), 1).astype(BF16)], axis=1)
        gather_received(*h_move)
        gather_received(*h_rim_move, h_next)

        @pl.when(h == nh - 1)
        def _():
            hgh[...] = jnp.zeros(hgh.shape, BF16)

        for f in range(2):
            hgat[f] = hgat[2]
            hgh[f] = hgh[2]
        for a in range(3):
            for b in range(3):
                pieces = [
                    hgh[2 * f + a, 0] if b + 2 * r == 4 else hgat[2 * f + a, b + 2 * r]
                    for f in range(nt)
                    for r in range(2)
                ]
                lhs = jnp.concatenate(pieces, axis=0)
                q = lax.dot_general(lhs, og_two, TN, preferred_element_type=F32)
                n = 64 * (a * 9 + b * 3)
                part4[n : n + 64] = q[0:64, 0:256]
                part4[n + 64 : n + 128] = q[64:128, 0:256]
                part4[n + 128 : n + 192] = q[0:64, 256:512]

    def coded(codes):
        code = codes[0]
        for k in range(1, nz):
            code = jnp.where(z == k, codes[k], code)
        return code

    chunk_code = coded(
        (0o1276534, 0o10276534, 0o21034576, 0o32451067,
         0o43526710, 0o56743201, 0o67543201, 0o76501243)
    )
    tap_code = coded((0o21, 0o21, 0o12, 0o102, 0o120, 0o210, 0o210, 0o201))

    def chunk_at(j):
        return chunk_code // 8**j % 8

    def tap_at(j):
        return tap_code // 8**j % 8

    def y_copies(i):
        two = pl.ds(2 * i, 2)
        return [
            send(
                sl.at[(y + k) % ny, two], r1.at[k - 1, two],
                rs1s.at[i, k - 1], rs1r.at[i, k - 1], at_y((y + k) % ny),
            )
            for k in (1, 3, 2)
        ]

    y_far = (y + 2) % ny

    def across_copy(j):
        c = chunk_at(j)
        k = (c - z + nz) % nz - 1
        where = (t, c * 2 + h % 2, d)
        return send(sl.at[y_far, j], q1.at[k], q1s.at[k], q1r.at[k], where)

    across_sum = send(q2, q3, q2s.at[0], q2r.at[0], at_y(y_far))

    def for_y(copies, act):
        for copy in copies[:2]:
            getattr(copy, act)()
        pl.when(core == 0)(getattr(copies[2], act))


    def send_chunks(i):
        def cut(m, carry):
            j, k = 2 * i + m // ny, m % ny
            c = chunk_at(j)
            n = groups * (c * ny + k)

            @pl.when(core == 0)
            def _():
                first_row = pl.multiple_of((n + 1 - chip // 2) // 2 * 8, 8)
                sl[k, j] = part[pl.ds(first_row, slot)].astype(BF16)

            @pl.when(core == 1)
            def _():
                first_row = pl.multiple_of((n + 3 - chip) // 4 * 8, 8)
                rows = part4[pl.ds(first_row, slot // 2)]
                stacked = jnp.concatenate([rows[:, :128], rows[:, 128:]], axis=0)
                sl[k, j] = stacked.astype(BF16)

            return carry

        lax.fori_loop(0, 2 * ny, cut, 0)
        for_y(y_copies(i), "start")

        @pl.when(core == 1)
        def _():
            for j in (2 * i, 2 * i + 1):
                if j < nz - 1:
                    across_copy(j).start()


    for k in range(3):

        @pl.when(core == 0)
        def _():
            a = tap_at(k)
            lhs = jnp.concatenate([xt[a + f] for f in range(2 * nt)], axis=1)
            q = jnp.dot(lhs, g3[...], preferred_element_type=F32)
            for b in range(3):
                for e in range(3):
                    n = pl.multiple_of(128 * (a * 9 + b * 3 + e), 128)
                    part[pl.ds(n, 128)] = q[128 * b : 128 * (b + 1), 128 * e : 128 * (e + 1)]

        send_chunks(k)
    send_chunks(3)
    h_rows.wait_recv()
    for c in g_rows:
        c.wait_recv()

    @pl.when(h == 0)
    def _():
        ge[0:2, 0] = jnp.zeros((2, 32, 256), BF16)

    @pl.when(h == nh - 1)
    def _():
        he[2:4, 4] = jnp.zeros((2, 32, 256), BF16)
        ge[0:2, 5] = jnp.zeros((2, 32, 256), BF16)

    h_frames.start()
    g_frames.start()


    def z_copy(j):
        c = chunk_at(j)
        k = (c - z + nz) % nz - 1
        where = (t, c * 2 + h % 2, d)
        return send(s1.at[c], r2.at[k], rs2s.at[k], rs2r.at[k], where)

    def pass_chunks(i):
        for_y(y_copies(i), "wait_recv")
        for j in (2 * i, 2 * i + 1):
            total = sl[y, j].astype(F32)
            for n in (0, 2):
                total = total + r1[n, j].astype(F32)
            total = total + jnp.where(core == 0, r1[1, j].astype(F32), 0.0)
            s1[chunk_at(j)] = total.astype(BF16)
            if j < nz - 1:
                z_copy(j).start()

    h_frames.wait_recv()

    @pl.when(first)
    def _():
        he[0] = he[2]
        he[1] = he[2]

    sums = [None] * 3
    for a in range(3):
        for b in range(3):
            for e in range(3):
                p = 16 * (e % 2)
                lhs = jnp.concatenate([he[a, b, p : p + 16], he[a, b + 2, p : p + 16]], axis=0)
                q = jnp.dot(lhs, w2[a * 9 + b * 3 + e], preferred_element_type=F32)
                sums[e] = q if sums[e] is None else sums[e] + q
    enc_ref[...] = (sums[0] + sums[1] + move_in_16(sums[2], -1)).astype(BF16)
    pass_chunks(0)
    pass_chunks(1)

    pass_chunks(2)
    pass_chunks(3)

    @pl.when(core == 1)
    def _():
        total = sl[y_far, nz - 1].astype(F32)
        for k in range(1, nz):
            source = ((z - k + nz) % nz * 2 + h % 2, d)
            send(
                sl.at[y_far, 0], q1.at[k - 1], q1s.at[k - 1], q1r.at[k - 1], (t, *source)
            ).wait_recv()
            total = total + q1[k - 1].astype(F32)
        q2[...] = total.astype(BF16)
        across_sum.start()

    g_frames.wait_recv()

    @pl.when(t == nt - 1)
    def _():
        ge[2:4] = jnp.zeros((2, 6, 32, 256), BF16)

    sums = [None] * 3
    for a in range(3):
        for b in range(3):
            lhs = ge[2 - a : 4 - a, 2 - b : 6 - b].reshape(256, 256)
            for e in range(3):
                q = lax.dot_general(lhs, w1[a * 9 + b * 3 + e], NT, preferred_element_type=F32)
                sums[e] = q if sums[e] is None else sums[e] + q
    for e in range(3):
        zs[e] = sums[e]

    @pl.when(first)
    def _():
        for e in range(3):
            total = zs[e, 0:128]
            for a, f in ((0, 0), (0, 1), (1, 0)):
                for b in range(3):
                    lhs = ge[f, 2 - b : 6 - b].reshape(128, 256)
                    total = total + lax.dot_general(
                        lhs, w1[a * 9 + b * 3 + e], NT, preferred_element_type=F32
                    )
            zs[e, 0:128] = total

    clip = (from_right(zs[0]) + zs[1] + from_left(zs[2])).astype(BF16)
    clip_ref[...] = lax.dot_general(
        by_column[...], clip, TN, preferred_element_type=F32
    ).astype(BF16)

    total = s1[z].astype(F32)
    for k in range(1, nz):
        source = ((z - k + nz) % nz * 2 + h % 2, d)
        send(
            s1.at[z], r2.at[k - 1], rs2s.at[k - 1], rs2r.at[k - 1], (t, *source)
        ).wait_recv()
        total = total + r2[k - 1].astype(F32)
    pl.when(core == 1)(across_sum.wait_recv)
    total = total + jnp.where(core == 1, q3[...].astype(F32), 0.0)
    fs[...] = total.astype(BF16)
    t_sends = []
    for k in range(1, nt):
        where = ((t + k) % nt, h, d)
        t_sends.append(send(fs, fg.at[t], ags.at[k - 1], agr.at[k - 1], where))
    for c in t_sends:
        c.start()
    fg[t] = fs[...]
    for k in range(1, nt):
        s = (t + nt - k) % nt
        send(fs, fg.at[s], ags.at[k - 1], agr.at[k - 1], (s, h, d)).wait_recv()

    for c in og_halo + x_halo + [h_rows] + g_rows + [h_frames, g_frames] + t_sends:
        c.wait_send()
    for i in range(nz // 2):
        for_y(y_copies(i), "wait_send")
    for j in range(nz - 1):
        z_copy(j).wait_send()

    @pl.when(core == 1)
    def _():
        for j in range(nz - 1):
            across_copy(j).wait_send()
        across_sum.wait_send()

    for move in (x_move, x_rim_move, g_move):
        gather_sent(0, *move)
    for move in (og_move, h_move):
        gather_sent(1, *move)
    gather_sent(1, *h_rim_move, h_prev)


def finish(sizes, enc_ref, clip_ref, fg, enc_hbm, clip_hbm, conv_hbm, down_hbm, ff, conv, down, sem):
    nt, nh, nd = sizes
    block = lax.axis_index("height") * nd + lax.axis_index("dp")
    groups = 864 // (nh * nd)
    slot = fg.shape[1]
    early = [
        pltpu.make_async_copy(enc_ref, enc_hbm, sem.at[0]),
        pltpu.make_async_copy(clip_ref, clip_hbm, sem.at[1]),
    ]
    for c in early:
        c.start()
    cells = nt * nh * nd * 256
    scale = (1.0 / math.sqrt(cells), 1.0 / math.sqrt(cells // 8))
    for s in range(nt):
        ff[s] = fg[s].astype(F32) * scale[s % 2]
    late = []
    for k, (out, hbm) in enumerate(((conv, conv_hbm), (down, down_hbm))):
        for j in range(groups):
            n = groups * block + j
            for o in range(2):
                if k == 0:
                    rows = ff[2 * (2 * (n % 2) + o), 8 * (j // 2) : 8 * (j // 2) + 8]
                else:
                    row = o * (slot // 2) + 8 * (j // 4)
                    rows = ff[2 * (n % 4) + 1, row : row + 8]
                out[8 * j : 8 * j + 8, 128 * o : 128 * o + 128] = rows
        c = pltpu.make_async_copy(out, hbm, sem.at[2 + k])
        c.start()
        late.append(c)
    for c in early + late:
        c.wait()


def body(mesh_sizes, video_clip, conv_weight, down_weight, output_grad):
    nt, nh, nd = mesh_sizes
    ny, nz = 2 * nd, nh // 2
    blocks = ny * nz
    groups = 864 // blocks
    slot = 8 * ((groups + 1) // 2)
    dma = pltpu.SemaphoreType.DMA

    def vm(*shape, dtype=BF16):
        return pltpu.VMEM(shape, dtype)

    scratch = [
        vm(256, 256), vm(256, 256), vm(512, 512), vm(256, 256), vm(32, 256), vm(27, 256, 256), vm(27, 256, 256),
        vm(4, 6, 32, 256), vm(2, 3, 16, 256), vm(4, 5, 32, 256), vm(4, 6, 32, 256),
        vm(2, 4, 32, 256, dtype=F32), vm(3, 256, 256, dtype=F32),
        vm(2, 2, 4, 32, 128), vm(2, 2, 2, 32, 128), vm(2, 2, 4, 32, 128),
        vm(4, 2, 4, 16, 128), vm(4, 2, 1, 16, 128),
        vm(2 * nt + 2, 4, 32, 128), vm(2 * nt + 2, 2, 32, 128), vm(2 * nt, 4, 32, 128),
        vm(2 * nt + 2, 4, 16, 128), vm(2 * nt + 2, 1, 16, 128), vm(nt, 2, 16, 256),
        vm(2 * nt + 2, 384, 128), vm(256 * nt, 384),
        vm(27 * 128 + 8, 128, dtype=F32), vm(27 * 64 + 8, 256, dtype=F32),
        vm(ny, nz, slot, 128), vm(ny - 1, nz, slot, 128),
        vm(nz, slot, 128), vm(nz - 1, slot, 128),
        vm(nz - 1, slot, 128), vm(slot, 128), vm(slot, 128),
        vm(slot, 128),
        dma((4,)), dma((8,)), dma((8,)), dma((5,)), dma((5,)),
    ]
    scratch += [dma((n,)) for _ in range(6) for n in (nt // 2, nt)]
    scratch += [dma(n) for n in ((nz // 2, ny - 1),) * 2 + ((nz - 1,),) * 4 + ((1,),) * 2 + ((nt - 1,),) * 2]
    vmem = pl.BlockSpec(memory_space=pltpu.VMEM)
    hbm = pl.BlockSpec(memory_space=pltpu.HBM)
    shape = jax.ShapeDtypeStruct
    features = (shape((32, 256), BF16), shape((256, 256), BF16))
    gathered = pl.pallas_call(
        functools.partial(kernel, mesh_sizes),
        out_shape=(*features, shape((nt, slot, 128), BF16)),
        in_specs=[hbm] * 4,
        out_specs=(vmem,) * 3,
        scratch_shapes=scratch,
        compiler_params=pltpu.CompilerParams(
            collective_id=0, has_side_effects=True, vmem_limit_bytes=44 * 2**20
        ),
    )(
        *(
            pltpu.with_memory_space_constraint(operand, pltpu.HBM)
            for operand in (
                video_clip.reshape(256, 256),
                conv_weight.reshape(27, 256, 256),
                down_weight.reshape(27, 256, 256),
                output_grad.reshape(32, 256),
            )
        )
    )
    rows = shape((groups * 8, 256), F32)
    enc, clip, conv, down = pl.pallas_call(
        functools.partial(finish, mesh_sizes),
        out_shape=(*features, rows, rows),
        in_specs=[vmem] * 3,
        out_specs=(hbm,) * 4,
        scratch_shapes=[
            vm(nt, slot, 128, dtype=F32),
            vm(groups * 8, 256, dtype=F32),
            vm(groups * 8, 256, dtype=F32),
            dma((4,)),
        ],
        compiler_params=pltpu.CompilerParams(vmem_limit_bytes=16 * 2**20),
    )(*gathered)
    return enc.reshape(1, 1, 2, 16, 256), clip.reshape(1, 2, 4, 32, 256), conv, down


def solution(mesh):
    sizes = tuple(mesh.shape[a] for a in ("tm", "height", "dp"))
    cells = P("dp", "tm", "height", None, None)
    rows = P(("height", "dp"), None)
    return jax.shard_map(
        functools.partial(body, sizes),
        mesh=mesh,
        in_specs=(cells, P(), P(), cells),
        out_specs=(cells, cells, rows, rows),
        check_vma=False,
    )
```

```python
import functools
import math

import jax
import jax.numpy as jnp
from jax import lax
from jax.experimental import pallas as pl
from jax.experimental.pallas import tpu as pltpu
from jax.sharding import PartitionSpec as P

MESH = pl.DeviceIdType.MESH
F32 = jnp.float32
BF16 = jnp.bfloat16
NT = (((1,), (1,)), ((), ()))
TN = (((0,), (0,)), ((), ()))


def iota2(shape, dim):
    return lax.broadcasted_iota(jnp.int32, shape, dim)


def one_hot(mask):
    return jnp.where(mask, 1.0, 0.0).astype(F32).astype(BF16)


def column_order(n):
    m, k = iota2((n, n), 0), iota2((n, n), 1)
    return one_hot(k == (m & ~31) + 2 * (m & 15) + ((m >> 4) & 1))


def channel_order(n):
    i, k = iota2((n, n), 0), iota2((n, n), 1)
    j = k & 127
    return one_hot(i == (j >> 3) * 16 + (k >> 7) * 8 + (j & 7))


def quarter_order(n):
    i, k = iota2((2 * n, 2 * n), 0), iota2((2 * n, 2 * n), 1)
    j = k & 63
    return one_hot(i == ((k >> 6) & 1) * n + (j >> 3) * 32 + (k >> 7) * 8 + (j & 7))


def move_in_16(x, step):
    n = x.shape[0]
    k = iota2(x.shape, 0) & 15
    rolled = pltpu.roll(x, step % n, 0)
    return jnp.where(k == (0 if step == 1 else 15), 0.0, rolled)


def halves(x):
    groups = x.shape[0] // 32
    parts = x.reshape(groups, 2, 16, x.shape[1])
    return parts[:, 0].reshape(groups * 16, -1), parts[:, 1].reshape(groups * 16, -1)


def joined(even, odd):
    groups = even.shape[0] // 16
    parts = [h.reshape(groups, 1, 16, h.shape[1]) for h in (even, odd)]
    return jnp.concatenate(parts, axis=1).reshape(groups * 32, -1)


def from_left(x):
    even, odd = halves(x)
    return joined(move_in_16(odd, 1), even)


def from_right(x):
    even, odd = halves(x)
    return joined(odd, move_in_16(even, -1))


def kernel(
    sizes,
    x_hbm, w1_hbm, w2_hbm, og_hbm,
    enc_ref, clip_ref, fg,
    by_column, by_channel, by_quarter, x_ref, og_ref, w1, w2, xe, oge, he, ge, hg, zs,
    xs, xsh, gs, hs, hsh, xg, xgh, gg, hgat, hgh, ogat, xt, g3, part, part4,
    sl, r1, s1, r2, q1, q2, q3, fs,
    wsem, p1s, p1r, p2s, p2r,
    xss, xsr, xhs, xhr, gss, gsr, hss, hsr, hhs, hhr, oss, osr,
    rs1s, rs1r, rs2s, rs2r, q1s, q1r, q2s, q2r, ags, agr,
):
    nt, nh, nd = sizes
    ny, nz = 2 * nd, nh // 2
    t, h, d = lax.axis_index("tm"), lax.axis_index("height"), lax.axis_index("dp")
    y, z = (h % 2) * nd + d, h // 2
    core, chip = t % 2, t // 2
    t_next, t_prev = (t + 1) % nt, (t + nt - 1) % nt
    h_next, h_prev = (h + 1) % nh, (h + nh - 1) % nh
    block = z * ny + y
    groups = 864 // (ny * nz)
    slot = 8 * ((groups + 1) // 2)

    wc1 = pltpu.make_async_copy(w1_hbm, w1, wsem.at[0])
    wc2 = pltpu.make_async_copy(w2_hbm, w2, wsem.at[1])
    first = t == 0
    og_in = pltpu.make_async_copy(og_hbm, og_ref, wsem.at[2])
    x_in = pltpu.make_async_copy(x_hbm, x_ref, wsem.at[3])
    for c in (x_in, og_in, wc2, wc1):
        c.start()

    def at_y(k):
        return (t, z * 2 + k // nd, k % nd)

    barrier = pltpu.get_barrier_semaphore()

    def greet(where):
        pl.semaphore_signal(barrier, inc=1, device_id=where, device_id_type=MESH)

    for k in range(1, nt):
        greet(((t + k) % nt, h, d))
    for k in range(nt // 2):
        greet((2 * k + 1, h_prev, d))

    @pl.when(core == 0)
    def _():
        greet((t, h_prev, d))
        for k in (t_prev, t, t_next):
            greet((k, h_next, d))

    @pl.when(core == 1)
    def _():
        greet((t_prev, h_prev, d))
        greet((t_next, h_prev, d))
        for k in range(nt):
            greet((k, h_next, d))

    for k in range(1, ny):
        greet(at_y((y + k) % ny))
    for k in range(1, nz):
        greet((t, ((z + k) % nz) * 2 + h % 2, d))

    by_column[...] = column_order(256)
    og_in.wait()
    x_in.wait()
    x_own = jnp.dot(by_column[...], x_ref[...], preferred_element_type=F32).astype(BF16)
    xe[2:4, 1:5] = x_own.reshape(2, 4, 32, 256)
    oge[0, 1:3] = og_ref[...].reshape(2, 16, 256)

    def keep_halves(block, out, rows):
        moved = jnp.dot(block, by_channel[...], preferred_element_type=F32).astype(BF16)
        for k in range(2):
            out[k] = moved[:, 128 * k : 128 * (k + 1)].reshape(2, rows, 32, 128)

    greetings = (nt - 1) + (ny - 1) + (nz - 1) + nt // 2 + 4
    pl.semaphore_wait(barrier, greetings + core * (nt - 2))

    def send(src, dst, ssem, rsem, where):
        return pltpu.make_async_remote_copy(
            src_ref=src, dst_ref=dst, send_sem=ssem, recv_sem=rsem, device_id=where, device_id_type=MESH
        )

    def p1(k, src, dst, where):
        return send(src, dst, p1s.at[k], p1r.at[k], where)

    og_halo = [
        p1(0, oge.at[0:1, 1:3], oge.at[1:2, 1:3], (t_prev, h, d)),
        p1(1, oge.at[0:1, 2:3], oge.at[0:1, 0:1], (t, h_next, d)),
        p1(2, oge.at[0:1, 2:3], oge.at[1:2, 0:1], (t_prev, h_next, d)),
    ]
    x_halo = [
        p1(3, xe.at[2:4, 1:5], xe.at[0:2, 1:5], (t_next, h, d)),
        p1(4, xe.at[2:4, 4:5], xe.at[2:4, 0:1], (t, h_next, d)),
        p1(5, xe.at[2:4, 1:2], xe.at[2:4, 5:6], (t, h_prev, d)),
        p1(6, xe.at[2:4, 4:5], xe.at[0:2, 0:1], (t_next, h_next, d)),
        p1(7, xe.at[2:4, 1:2], xe.at[0:2, 5:6], (t_next, h_prev, d)),
    ]
    for c in og_halo + x_halo:
        c.start()

    def gather_sends(role, source, target, ssem, rsem, to_h=None):
        rim = to_h is not None
        to_h = to_h if rim else h
        for k in (2, 1, 3, 0):
            to_chip = (chip + k) % (nt // 2)
            to = to_chip * 2 + role
            c = send(source(to_chip), target(t), ssem.at[k], rsem.at[t], (to, to_h, d))
            if k == 0 and not rim:
                pl.when(core != role)(c.start)
            else:
                c.start()

    def gather_sent(role, source, target, ssem, rsem, to_h=None):
        rim = to_h is not None
        to_h = to_h if rim else h
        for k in (2, 1, 3, 0):
            to_chip = (chip + k) % (nt // 2)
            to = to_chip * 2 + role
            c = send(source(to_chip), target(t), ssem.at[k], rsem.at[t], (to, to_h, d))
            if k == 0 and not rim:
                pl.when(core != role)(c.wait_send)
            else:
                c.wait_send()

    def gather_received(source, target, ssem, rsem, from_h=None):
        for k in range(0 if from_h is not None else 1, nt):
            s = (t + k) % nt
            where = (s, h if from_h is None else from_h, d)
            send(source(0), target(s), ssem.at[0], rsem.at[s], where).wait_recv()

    def later_frames(ref):
        return lambda s: ref.at[pl.ds(2 + 2 * s, 2)]

    og_move = (lambda c: oge.at[0, 1:3], lambda s: ogat.at[s], oss, osr)
    x_move = (lambda c: xs.at[c // 2], later_frames(xg), xss, xsr)
    x_rim_move = (lambda c: xsh.at[c // 2], later_frames(xgh), xhs, xhr)
    g_move = (lambda c: gs.at[c % 2], lambda s: gg.at[pl.ds(2 * s, 2)], gss, gsr)
    h_move = (lambda c: hs.at[c], later_frames(hgat), hss, hsr)
    h_rim_move = (lambda c: hsh.at[c], later_frames(hgh), hhs, hhr)
    gather_sends(1, *og_move)

    by_channel[...] = channel_order(256)
    keep_halves(x_own, xs, 4)
    by_quarter[...] = quarter_order(256)
    part[pl.ds(27 * 128, 8)] = jnp.zeros((8, 128), F32)
    part4[pl.ds(27 * 64, 8)] = jnp.zeros((8, 256), F32)
    for c in og_halo:
        c.wait_recv()
    gather_sends(0, *x_move)

    wc2.wait()

    @pl.when(t == nt - 1)
    def _():
        oge[1] = jnp.zeros((3, 16, 256), BF16)

    @pl.when(h == 0)
    def _():
        oge[:, 0] = jnp.zeros((2, 16, 256), BF16)

    og_rows = oge[...].reshape(96, 256)
    terms = {}
    for e in range(3):
        for a in range(3):
            for b in range(3):
                lhs = og_rows if a < 2 else og_rows[:48]
                q = lax.dot_general(lhs, w2[a * 9 + b * 3 + e], NT, preferred_element_type=F32)
                offset = 0 if b == 2 else 16
                here = q[offset : offset + 32]
                if a < 2:
                    here = jnp.where(first, here, 0.0)
                    later = q[48 + offset : 48 + offset + 32]
                    key = (a, b % 2, e)
                    terms[key] = terms.get(key, 0.0) + later
                key = (0, b % 2, e)
                terms[key] = terms.get(key, 0.0) + here
    for f in range(2):
        for b in range(2):
            even = terms[f, b, 0] + move_in_16(terms[f, b, 2], 1)
            odd = terms[f, b, 1]
            for u in range(2):
                hg[f, 2 * u + b, 0:16] = even[16 * u : 16 * u + 16]
                hg[f, 2 * u + b, 16:32] = odd[16 * u : 16 * u + 16]

    for c in x_halo:
        c.wait_recv()

    @pl.when(h == 0)
    def _():
        xe[:, 0] = jnp.zeros((4, 32, 256), BF16)

    @pl.when(h == nh - 1)
    def _():
        xe[:, 5] = jnp.zeros((4, 32, 256), BF16)

    @pl.when(first)
    def _():
        xe[0] = xe[2]
        xe[1] = xe[2]

    rims = jnp.concatenate([xe[2:4, 0:1], xe[2:4, 5:6]], axis=1)
    keep_halves(rims.reshape(128, 256), xsh, 2)
    gather_sends(0, *x_rim_move)

    wc1.wait()
    sums = [None] * 3
    for a in range(3):
        for b in range(3):
            lhs = xe[a : a + 2, b : b + 4].reshape(256, 256)
            for e in range(3):
                q = jnp.dot(lhs, w1[a * 9 + b * 3 + e], preferred_element_type=F32)
                sums[e] = q if sums[e] is None else sums[e] + q
    value = from_left(sums[0]) + sums[1] + from_right(sums[2])
    sigmoid = jax.nn.sigmoid(value)
    he[2:4, 0:4] = (value * sigmoid).astype(BF16).reshape(2, 4, 32, 256)
    zs[0] = sigmoid * (1.0 + value * (1.0 - sigmoid))

    def p2(k, src, dst, where):
        return send(src, dst, p2s.at[k], p2r.at[k], where)

    h_rows = p2(0, he.at[2:4, 0:1], he.at[2:4, 4:5], (t, h_prev, d))
    g_rows = [
        p2(1, ge.at[0:2, 4:5], ge.at[0:2, 0:1], (t, h_next, d)),
        p2(2, ge.at[0:2, 1:2], ge.at[0:2, 5:6], (t, h_prev, d)),
    ]
    h_frames = p2(3, he.at[2:4], he.at[0:2], (t_next, h, d))
    g_frames = p2(4, ge.at[0:2], ge.at[2:4], (t_prev, h, d))
    def keep_quarters(block, out, rows):
        lanes = [block[..., p : p + 16, :].reshape(32 * rows, 256) for p in (0, 16)]
        both = jnp.concatenate(lanes, axis=1)
        moved = jnp.dot(both, by_quarter[...], preferred_element_type=F32).astype(BF16)
        for k in range(4):
            out[k] = moved[:, 128 * k : 128 * (k + 1)].reshape(2, rows, 16, 128)

    for f in (1, 0):
        grad = (hg[f].reshape(128, 256) * zs[0, 128 * f : 128 * f + 128]).astype(BF16)
        ge[f, 1:5] = grad.reshape(4, 32, 256)
        for k in range(2):
            gs[k, f] = grad[:, 128 * k : 128 * (k + 1)].reshape(4, 32, 128)
    gather_sends(0, *g_move)
    keep_quarters(he[2:4, 0:4], hs, 4)
    for k in range(4):
        hsh[k] = hs[k, :, 0:1]
    gather_sends(1, *h_rim_move, h_prev)
    gather_sends(1, *h_move)
    h_rows.start()
    for c in g_rows:
        c.start()

    @pl.when(core == 0)
    def _():
        xg[pl.ds(2 + 2 * t, 2)] = xs[chip // 2]
        xgh[pl.ds(2 + 2 * t, 2)] = xsh[chip // 2]
        gg[pl.ds(2 * t, 2)] = gs[chip % 2]
        gather_received(*x_move)
        gather_received(*x_rim_move)
        for f in range(2):
            xg[f] = xg[2]
            xgh[f] = xgh[2]

        def turn(f, carry):
            rows = jnp.concatenate([xgh[f, 0:1], xg[f], xgh[f, 1:2]], axis=0)
            for b in range(3):
                xt[f, 128 * b : 128 * (b + 1)] = rows[b : b + 4].reshape(128, 128).T
            return carry

        lax.fori_loop(0, 2 * nt + 2, turn, 0)
        gather_received(*g_move)

        def spread(s, carry):
            rows = pl.ds(pl.multiple_of(256 * s, 256), 256)
            g = gg[pl.ds(2 * s, 2)].reshape(256, 128)
            wide = g.astype(F32)
            g3[rows, 0:128] = from_right(wide).astype(BF16)
            g3[rows, 128:256] = g
            g3[rows, 256:384] = from_left(wide).astype(BF16)
            return carry

        lax.fori_loop(0, nt, spread, 0)

    @pl.when(core == 1)
    def _():
        hgat[pl.ds(2 + 2 * t, 2)] = hs[chip]
        ogat[t] = oge[0, 1:3]
        gather_received(*og_move)
        og_all = ogat[...].reshape(32 * nt, 256)
        og_two = jnp.concatenate([og_all, move_in_16(og_all.astype(F32), 1).astype(BF16)], axis=1)
        gather_received(*h_move)
        gather_received(*h_rim_move, h_next)

        @pl.when(h == nh - 1)
        def _():
            hgh[...] = jnp.zeros(hgh.shape, BF16)

        for f in range(2):
            hgat[f] = hgat[2]
            hgh[f] = hgh[2]
        for a in range(3):
            for b in range(3):
                pieces = [
                    hgh[2 * f + a, 0] if b + 2 * r == 4 else hgat[2 * f + a, b + 2 * r]
                    for f in range(nt)
                    for r in range(2)
                ]
                lhs = jnp.concatenate(pieces, axis=0)
                q = lax.dot_general(lhs, og_two, TN, preferred_element_type=F32)
                n = 64 * (a * 9 + b * 3)
                part4[n : n + 64] = q[0:64, 0:256]
                part4[n + 64 : n + 128] = q[64:128, 0:256]
                part4[n + 128 : n + 192] = q[0:64, 256:512]

    def coded(codes):
        code = codes[0]
        for k in range(1, nz):
            code = jnp.where(z == k, codes[k], code)
        return code

    chunk_code = coded(
        (0o1276534, 0o10276534, 0o21034576, 0o32451067,
         0o43526710, 0o56743201, 0o67543201, 0o76501243)
    )
    tap_code = coded((0o21, 0o21, 0o12, 0o102, 0o120, 0o210, 0o210, 0o201))

    def chunk_at(j):
        return chunk_code // 8**j % 8

    def tap_at(j):
        return tap_code // 8**j % 8

    def y_copies(i):
        two = pl.ds(2 * i, 2)
        return [
            send(
                sl.at[(y + k) % ny, two], r1.at[k - 1, two],
                rs1s.at[i, k - 1], rs1r.at[i, k - 1], at_y((y + k) % ny),
            )
            for k in (1, 3, 2)
        ]

    y_far = (y + 2) % ny

    def across_copy(j):
        c = chunk_at(j)
        k = (c - z + nz) % nz - 1
        where = (t, c * 2 + h % 2, d)
        return send(sl.at[y_far, j], q1.at[k], q1s.at[k], q1r.at[k], where)

    across_sum = send(q2, q3, q2s.at[0], q2r.at[0], at_y(y_far))

    def for_y(copies, act):
        for copy in copies[:2]:
            getattr(copy, act)()
        pl.when(core == 0)(getattr(copies[2], act))


    def send_chunks(i):
        def cut(m, carry):
            j, k = 2 * i + m // ny, m % ny
            c = chunk_at(j)
            n = groups * (c * ny + k)

            @pl.when(core == 0)
            def _():
                first_row = pl.multiple_of((n + 1 - chip // 2) // 2 * 8, 8)
                sl[k, j] = part[pl.ds(first_row, slot)].astype(BF16)

            @pl.when(core == 1)
            def _():
                first_row = pl.multiple_of((n + 3 - chip) // 4 * 8, 8)
                rows = part4[pl.ds(first_row, slot // 2)]
                stacked = jnp.concatenate([rows[:, :128], rows[:, 128:]], axis=0)
                sl[k, j] = stacked.astype(BF16)

            return carry

        lax.fori_loop(0, 2 * ny, cut, 0)
        for_y(y_copies(i), "start")

        @pl.when(core == 1)
        def _():
            for j in (2 * i, 2 * i + 1):
                if j < nz - 1:
                    across_copy(j).start()


    for k in range(3):

        @pl.when(core == 0)
        def _():
            a = tap_at(k)
            lhs = jnp.concatenate([xt[a + f] for f in range(2 * nt)], axis=1)
            q = jnp.dot(lhs, g3[...], preferred_element_type=F32)
            for b in range(3):
                for e in range(3):
                    n = pl.multiple_of(128 * (a * 9 + b * 3 + e), 128)
                    part[pl.ds(n, 128)] = q[128 * b : 128 * (b + 1), 128 * e : 128 * (e + 1)]

        send_chunks(k)
    send_chunks(3)
    h_rows.wait_recv()
    for c in g_rows:
        c.wait_recv()

    @pl.when(h == 0)
    def _():
        ge[0:2, 0] = jnp.zeros((2, 32, 256), BF16)

    @pl.when(h == nh - 1)
    def _():
        he[2:4, 4] = jnp.zeros((2, 32, 256), BF16)
        ge[0:2, 5] = jnp.zeros((2, 32, 256), BF16)

    h_frames.start()
    g_frames.start()


    def z_copy(j):
        c = chunk_at(j)
        k = (c - z + nz) % nz - 1
        where = (t, c * 2 + h % 2, d)
        return send(s1.at[c], r2.at[k], rs2s.at[k], rs2r.at[k], where)

    def pass_chunks(i):
        for_y(y_copies(i), "wait_recv")
        for j in (2 * i, 2 * i + 1):
            total = sl[y, j].astype(F32)
            for n in (0, 2):
                total = total + r1[n, j].astype(F32)
            total = total + jnp.where(core == 0, r1[1, j].astype(F32), 0.0)
            s1[chunk_at(j)] = total.astype(BF16)
            if j < nz - 1:
                z_copy(j).start()

    h_frames.wait_recv()

    @pl.when(first)
    def _():
        he[0] = he[2]
        he[1] = he[2]

    sums = [None] * 3
    for a in range(3):
        for b in range(3):
            for e in range(3):
                p = 16 * (e % 2)
                lhs = jnp.concatenate([he[a, b, p : p + 16], he[a, b + 2, p : p + 16]], axis=0)
                q = jnp.dot(lhs, w2[a * 9 + b * 3 + e], preferred_element_type=F32)
                sums[e] = q if sums[e] is None else sums[e] + q
    enc_ref[...] = (sums[0] + sums[1] + move_in_16(sums[2], -1)).astype(BF16)
    pass_chunks(0)
    pass_chunks(1)

    pass_chunks(2)
    pass_chunks(3)

    @pl.when(core == 1)
    def _():
        total = sl[y_far, nz - 1].astype(F32)
        for k in range(1, nz):
            source = ((z - k + nz) % nz * 2 + h % 2, d)
            send(
                sl.at[y_far, 0], q1.at[k - 1], q1s.at[k - 1], q1r.at[k - 1], (t, *source)
            ).wait_recv()
            total = total + q1[k - 1].astype(F32)
        q2[...] = total.astype(BF16)
        across_sum.start()

    g_frames.wait_recv()

    @pl.when(t == nt - 1)
    def _():
        ge[2:4] = jnp.zeros((2, 6, 32, 256), BF16)

    sums = [None] * 3
    for a in range(3):
        for b in range(3):
            lhs = ge[2 - a : 4 - a, 2 - b : 6 - b].reshape(256, 256)
            for e in range(3):
                q = lax.dot_general(lhs, w1[a * 9 + b * 3 + e], NT, preferred_element_type=F32)
                sums[e] = q if sums[e] is None else sums[e] + q
    for e in range(3):
        zs[e] = sums[e]

    @pl.when(first)
    def _():
        for e in range(3):
            total = zs[e, 0:128]
            for a, f in ((0, 0), (0, 1), (1, 0)):
                for b in range(3):
                    lhs = ge[f, 2 - b : 6 - b].reshape(128, 256)
                    total = total + lax.dot_general(
                        lhs, w1[a * 9 + b * 3 + e], NT, preferred_element_type=F32
                    )
            zs[e, 0:128] = total

    clip = (from_right(zs[0]) + zs[1] + from_left(zs[2])).astype(BF16)
    clip_ref[...] = lax.dot_general(
        by_column[...], clip, TN, preferred_element_type=F32
    ).astype(BF16)

    total = s1[z].astype(F32)
    for k in range(1, nz):
        source = ((z - k + nz) % nz * 2 + h % 2, d)
        send(
            s1.at[z], r2.at[k - 1], rs2s.at[k - 1], rs2r.at[k - 1], (t, *source)
        ).wait_recv()
        total = total + r2[k - 1].astype(F32)
    pl.when(core == 1)(across_sum.wait_recv)
    total = total + jnp.where(core == 1, q3[...].astype(F32), 0.0)
    fs[...] = total.astype(BF16)
    steps = [(k, n) for k in (2, 1, 3) for n in (0, 1)] + [(0, 1)]

    def t_copy(i, sign, slot_of):
        k, n = steps[i]
        other = (chip + sign * k + nt // 2) % (nt // 2) * 2 + (core + n) % 2
        return send(fs, fg.at[slot_of(other)], ags.at[i], agr.at[i], (other, h, d))

    t_sends = [t_copy(i, 1, lambda other: t) for i in range(nt - 1)]
    for c in t_sends:
        c.start()
    fg[t] = fs[...]
    for i in range(nt - 1):
        t_copy(i, -1, lambda other: other).wait_recv()

    for c in og_halo + x_halo + [h_rows] + g_rows + [h_frames, g_frames] + t_sends:
        c.wait_send()
    for i in range(nz // 2):
        for_y(y_copies(i), "wait_send")
    for j in range(nz - 1):
        z_copy(j).wait_send()

    @pl.when(core == 1)
    def _():
        for j in range(nz - 1):
            across_copy(j).wait_send()
        across_sum.wait_send()

    for move in (x_move, x_rim_move, g_move):
        gather_sent(0, *move)
    for move in (og_move, h_move):
        gather_sent(1, *move)
    gather_sent(1, *h_rim_move, h_prev)


def finish(sizes, enc_ref, clip_ref, fg, enc_hbm, clip_hbm, conv_hbm, down_hbm, ff, conv, down, sem):
    nt, nh, nd = sizes
    block = lax.axis_index("height") * nd + lax.axis_index("dp")
    groups = 864 // (nh * nd)
    slot = fg.shape[1]
    early = [
        pltpu.make_async_copy(enc_ref, enc_hbm, sem.at[0]),
        pltpu.make_async_copy(clip_ref, clip_hbm, sem.at[1]),
    ]
    for c in early:
        c.start()
    cells = nt * nh * nd * 256
    scale = (1.0 / math.sqrt(cells), 1.0 / math.sqrt(cells // 8))
    for s in range(nt):
        ff[s] = fg[s].astype(F32) * scale[s % 2]
    late = []
    for k, (out, hbm) in enumerate(((conv, conv_hbm), (down, down_hbm))):
        for j in range(groups):
            n = groups * block + j
            for o in range(2):
                if k == 0:
                    rows = ff[2 * (2 * (n % 2) + o), 8 * (j // 2) : 8 * (j // 2) + 8]
                else:
                    row = o * (slot // 2) + 8 * (j // 4)
                    rows = ff[2 * (n % 4) + 1, row : row + 8]
                out[8 * j : 8 * j + 8, 128 * o : 128 * o + 128] = rows
        c = pltpu.make_async_copy(out, hbm, sem.at[2 + k])
        c.start()
        late.append(c)
    for c in early + late:
        c.wait()


def body(mesh_sizes, video_clip, conv_weight, down_weight, output_grad):
    nt, nh, nd = mesh_sizes
    ny, nz = 2 * nd, nh // 2
    blocks = ny * nz
    groups = 864 // blocks
    slot = 8 * ((groups + 1) // 2)
    dma = pltpu.SemaphoreType.DMA

    def vm(*shape, dtype=BF16):
        return pltpu.VMEM(shape, dtype)

    scratch = [
        vm(256, 256), vm(256, 256), vm(512, 512), vm(256, 256), vm(32, 256), vm(27, 256, 256), vm(27, 256, 256),
        vm(4, 6, 32, 256), vm(2, 3, 16, 256), vm(4, 5, 32, 256), vm(4, 6, 32, 256),
        vm(2, 4, 32, 256, dtype=F32), vm(3, 256, 256, dtype=F32),
        vm(2, 2, 4, 32, 128), vm(2, 2, 2, 32, 128), vm(2, 2, 4, 32, 128),
        vm(4, 2, 4, 16, 128), vm(4, 2, 1, 16, 128),
        vm(2 * nt + 2, 4, 32, 128), vm(2 * nt + 2, 2, 32, 128), vm(2 * nt, 4, 32, 128),
        vm(2 * nt + 2, 4, 16, 128), vm(2 * nt + 2, 1, 16, 128), vm(nt, 2, 16, 256),
        vm(2 * nt + 2, 384, 128), vm(256 * nt, 384),
        vm(27 * 128 + 8, 128, dtype=F32), vm(27 * 64 + 8, 256, dtype=F32),
        vm(ny, nz, slot, 128), vm(ny - 1, nz, slot, 128),
        vm(nz, slot, 128), vm(nz - 1, slot, 128),
        vm(nz - 1, slot, 128), vm(slot, 128), vm(slot, 128),
        vm(slot, 128),
        dma((4,)), dma((8,)), dma((8,)), dma((5,)), dma((5,)),
    ]
    scratch += [dma((n,)) for _ in range(6) for n in (nt // 2, nt)]
    scratch += [dma(n) for n in ((nz // 2, ny - 1),) * 2 + ((nz - 1,),) * 4 + ((1,),) * 2 + ((nt - 1,),) * 2]
    vmem = pl.BlockSpec(memory_space=pltpu.VMEM)
    hbm = pl.BlockSpec(memory_space=pltpu.HBM)
    shape = jax.ShapeDtypeStruct
    features = (shape((32, 256), BF16), shape((256, 256), BF16))
    gathered = pl.pallas_call(
        functools.partial(kernel, mesh_sizes),
        out_shape=(*features, shape((nt, slot, 128), BF16)),
        in_specs=[hbm] * 4,
        out_specs=(vmem,) * 3,
        scratch_shapes=scratch,
        compiler_params=pltpu.CompilerParams(
            collective_id=0, has_side_effects=True, vmem_limit_bytes=44 * 2**20
        ),
    )(
        *(
            pltpu.with_memory_space_constraint(operand, pltpu.HBM)
            for operand in (
                video_clip.reshape(256, 256),
                conv_weight.reshape(27, 256, 256),
                down_weight.reshape(27, 256, 256),
                output_grad.reshape(32, 256),
            )
        )
    )
    rows = shape((groups * 8, 256), F32)
    enc, clip, conv, down = pl.pallas_call(
        functools.partial(finish, mesh_sizes),
        out_shape=(*features, rows, rows),
        in_specs=[vmem] * 3,
        out_specs=(hbm,) * 4,
        scratch_shapes=[
            vm(nt, slot, 128, dtype=F32),
            vm(groups * 8, 256, dtype=F32),
            vm(groups * 8, 256, dtype=F32),
            dma((4,)),
        ],
        compiler_params=pltpu.CompilerParams(vmem_limit_bytes=16 * 2**20),
    )(*gathered)
    return enc.reshape(1, 1, 2, 16, 256), clip.reshape(1, 2, 4, 32, 256), conv, down


def solution(mesh):
    sizes = tuple(mesh.shape[a] for a in ("tm", "height", "dp"))
    cells = P("dp", "tm", "height", None, None)
    rows = P(("height", "dp"), None)
    return jax.shard_map(
        functools.partial(body, sizes),
        mesh=mesh,
        in_specs=(cells, P(), P(), cells),
        out_specs=(cells, cells, rows, rows),
        check_vma=False,
    )
```
